32 devices in a mesh: groups: 2 (over y), fil: 4 (over z), col: 4 (over x, core).
Axes of the slice: x: 2, y: 2, z: 4, core: 2. Of those that a mesh axis runs over, the one named last changes fastest.
Arguments:
- geometry: float32 [6, 6144], P(None, ('groups', 'fil', 'col')), parts along dimension 1, may hold values from -4 to 4, as said below
- net_ids: int32 [6144], P(('groups', 'fil', 'col')), parts along dimension 0, may hold values from 0 to 3
- layers: int32 [6144], P(('groups', 'fil', 'col')), parts along dimension 0, may hold values from 0 to 7
- trial_modes: bfloat16 [6144, 32], P(('groups', 'fil', 'col')), parts along dimension 0, may hold values from -6 to 6
- low_edge: float32 [2], P('groups'), parts along dimension 0, may hold values from 1 to 3
- high_edge: float32 [2], P('groups'), parts along dimension 0, may hold values from 40 to 80
Outputs:
- ritz_basis: float32 [6144, 32], P(('groups', 'fil', 'col')), parts along dimension 0
- projected: float32 [64, 32], P('groups'), parts along dimension 0
The draws below stay inside these ranges and needn't reach their ends.
There are 2 independent parts, one for each index of `groups`. The reference program is written for one: setup_inputs(seed, part) draws one part's arguments, and reference() takes and returns one part's arrays. A program takes and returns all parts, laid end to end along the dimension named above; each array names one. Nothing has to cross between parts.
Inputs may be any that keep to these rules, and one draw needn't show every extreme that they name: `geometry`: rows 0 and 1 lie in [0, 1]; row 5 lies in [0.002, 0.006].
All inputs are finite; a program needn't handle non-finite values.
Results may differ from the reference program's by a relative error of at most 0.00055.
The reference program's roundings to bfloat16 on the way count: a program that leaves them out, or rounds other values in their place, can miss the bound.
Values may be sent and summed in bfloat16 or wider, within the bound.
No kernel may reach another device: no remote copies, remote signals or barrier semaphores. Data moves between devices by JAX's collectives and lax.ppermute only.
A program may use at most 64 MiB of HBM per device.

```python
import math
import jax
import jax.numpy as jnp
from jax import lax

K = 32
LAYERS = 8
NETS = 4
N = 3072


def draw_geometry(key, part):
    key = jax.random.fold_in(key, 11)
    subkeys = jax.random.split(key, 3)
    in_plane = jax.random.uniform(subkeys[0], (2, N), jnp.float32)
    segment = jax.random.truncated_normal(subkeys[1], -4.0, 4.0, (3, N), jnp.float32)
    radius = 0.002 * jnp.exp(jnp.log(3.0) * jax.random.uniform(subkeys[2], (1, N), jnp.float32))
    return jnp.concatenate([in_plane, segment, radius], axis=0)


def plant(values, stream_key, smallest, high):
    dims = values.shape
    place = [jax.random.randint(jax.random.fold_in(stream_key, axis), (), 0, dims[axis]) for axis in range(len(dims))]
    values = values.at[tuple(place)].set(smallest)
    longest = dims.index(max(dims))
    place[longest] = (place[longest] + 1) % dims[longest]
    return values.at[tuple(place)].set(high)


def block_scale(stream_key, shape, cuts, smallest, top_value):
    def one(position, parts):
        steps = jax.random.uniform(jax.random.fold_in(jax.random.fold_in(stream_key, 6), position), (parts,), jnp.float32, smallest / len(cuts), top_value / len(cuts))
        return jnp.repeat(jnp.exp(steps), shape[position] // parts).reshape((-1,) + (1,) * (len(shape) - position - 1))

    factor_of = one(*cuts[0])
    for cut in cuts[1:]:
        factor_of = factor_of * one(*cut)
    return factor_of


def noise(key, extent, scale, limit, cuts=(), kind=jnp.bfloat16):
    values = jax.random.normal(key, extent, jnp.float32) * scale
    if len(cuts) > 0:
        values = block_scale(key, extent, cuts, -0.22, 0.18) * values
    return jnp.clip(values, min=-limit, max=limit).astype(kind)


def setup_inputs(seed: int = 0, part: int = 0) -> dict:
    splits = jax.random.split(jax.random.key(seed), 7)
    own_keys = jax.random.split(jax.random.fold_in(splits[6], part), 7)
    geometry = draw_geometry(jax.random.fold_in(jax.random.fold_in(splits[6], part), 71), part)
    net_ids = plant(jax.random.randint(own_keys[1], (N,), 0, NETS), jax.random.fold_in(own_keys[1], 1), 0, NETS - 1).astype(jnp.int32)
    layers = plant(jax.random.randint(own_keys[2], (N,), 0, LAYERS), jax.random.fold_in(own_keys[2], 1), 0, LAYERS - 1).astype(jnp.int32)
    trial_modes = noise(own_keys[3], (N, K), 1.0, 6.0, ((0, 16),))
    low_edge = jnp.clip(jax.random.uniform(own_keys[4], (1,), jnp.float32, 1.0, 3.0), 1.0, 3.0)
    high_edge = jnp.clip(jax.random.uniform(own_keys[5], (1,), jnp.float32, 40.0, 80.0), 40.0, 80.0)
    return dict(geometry=geometry, net_ids=net_ids, layers=layers, trial_modes=trial_modes, low_edge=low_edge, high_edge=high_edge)


SHIELD_FACTOR = 0.5
LAYER_PITCH = 0.02

def features(geometry, net_ids, layers):
    height = layers.astype(jnp.float32) * LAYER_PITCH
    return jnp.stack([geometry[0], geometry[1], height, geometry[2], geometry[3], geometry[4], geometry[5], net_ids.astype(jnp.float32)], axis=0)

def kernel_tile(row_feat, col_feat, kernel_scale):
    delta_x = row_feat[0][:, None] - col_feat[0][None, :]
    delta_y = row_feat[1][:, None] - col_feat[1][None, :]
    delta_z = row_feat[2][:, None] - col_feat[2][None, :]
    radius_sq = row_feat[6][:, None] * row_feat[6][:, None] + col_feat[6][None, :] * col_feat[6][None, :]
    spread = delta_x * delta_x + delta_y * delta_y + delta_z * delta_z + radius_sq
    alignment = row_feat[3][:, None] * col_feat[3][None, :] + row_feat[4][:, None] * col_feat[4][None, :] + row_feat[5][:, None] * col_feat[5][None, :]
    couple = jnp.where(row_feat[7][:, None] == col_feat[7][None, :], 1.0, SHIELD_FACTOR)
    return (alignment * couple * lax.rsqrt(spread) * kernel_scale).astype(jnp.bfloat16)

def reference(geometry, net_ids, layers, trial_modes, low_edge, high_edge):
    filament_feats = features(geometry, net_ids, layers)
    kernel_scale = 1.0 / math.sqrt(N)
    panel_rows = math.gcd(N, 512)

    def apply_operator(mode_block):

        def row_panel(offset):
            row_feat = lax.dynamic_slice_in_dim(filament_feats, offset, panel_rows, 1)
            tile_vals = kernel_tile(row_feat, filament_feats, kernel_scale)
            return jnp.dot(tile_vals.astype(jnp.float32), mode_block.astype(jnp.float32), preferred_element_type=jnp.float32)
        row_starts = (jnp.arange(N // panel_rows) * panel_rows).astype(jnp.int32)
        return lax.map(row_panel, row_starts).reshape(N, mode_block.shape[1])
    centre = (low_edge[0] + high_edge[0]) * 0.5
    half_width = (high_edge[0] - low_edge[0]) * 0.5
    filtered_one = ((apply_operator(trial_modes) - centre * trial_modes.astype(jnp.float32)) / half_width).astype(jnp.bfloat16)
    second = 2.0 * (apply_operator(filtered_one) - centre * filtered_one.astype(jnp.float32)) / half_width - trial_modes.astype(jnp.float32)
    second_low = second.astype(jnp.bfloat16)
    image_block = apply_operator(second_low)
    gram_matrix = jnp.dot(second.T, second, precision=lax.Precision.HIGHEST) / N
    cross_matrix = jnp.dot(second.T, image_block, precision=lax.Precision.HIGHEST) / N
    factor = jnp.linalg.cholesky(gram_matrix)
    ritz_basis = jax.scipy.linalg.solve_triangular(factor, second.T, lower=True).T
    half_solved = jax.scipy.linalg.solve_triangular(factor, cross_matrix, lower=True)
    projected = jax.scipy.linalg.solve_triangular(factor, half_solved.T, lower=True).T
    return (ritz_basis, projected)
```

```python
import functools
import math

import jax
import jax.numpy as jnp
from jax import lax
from jax.experimental import pallas as pl
from jax.experimental.pallas import tpu as pltpu
from jax.sharding import PartitionSpec as P

SHIELD_FACTOR = 0.5
LAYER_PITCH = 0.02
NETS = 4
LAYERS = 8
F32 = jnp.float32
BF16 = jnp.bfloat16
HIGHEST = lax.Precision.HIGHEST
VMEM_SPEC = pl.BlockSpec(memory_space=pltpu.VMEM)
SMEM_SPEC = pl.BlockSpec(memory_space=pltpu.SMEM)
PAYLOAD_ROWS = 64
TILE_ROWS = 256
TILE_COLS = 512


def pieces(x):
    high = x.astype(BF16).astype(F32)
    mid = (x - high).astype(BF16).astype(F32)
    low = (x - high - mid).astype(BF16).astype(F32)
    return high, mid, low


def pack_body(geometry, nets, layers, modes, out):
    shape = (1, geometry.shape[1])
    high, mid, low = pieces(geometry[...])
    zeros = jnp.zeros((2,) + shape[1:], F32)
    rest = jnp.zeros((8,) + shape[1:], F32)
    rows = jnp.concatenate(
        [high, nets[...].astype(F32), layers[...].astype(F32), mid, zeros, low, zeros, rest], axis=0
    ).astype(BF16)
    for place in range(out.shape[0]):
        out[place, 0:32, :] = modes[...]
        out[place, 32:64, :] = rows


def tile_body(scale, own, other, low_edge, high_edge, panel, filtered, stage, left, right, coarse, xy, total):
    count, _, width = own.shape
    cols = count * width
    rows = 2 * cols
    for half, part in enumerate((own, other)):
        for place in range(count):
            start = half * cols + place * width
            stage[:, start : start + width] = part[place].astype(F32)

    def rows_of(first, last, length):
        return stage[first:last, 0:length]

    def groups(base, nets):
        listed = [base] + [jnp.where(nets == float(n), base, 0.0) for n in range(NETS)]
        return jnp.concatenate(listed, axis=0)

    def squares(length):
        return pieces(jnp.square(rows_of(37, 38, length) + rows_of(45, 46, length) + rows_of(53, 54, length)))

    nets = rows_of(38, 39, rows)
    segment = [groups(rows_of(s + 2, s + 5, rows), nets) for s in (32, 40, 48)]
    place_x = [rows_of(s, s + 1, rows) for s in (32, 40, 48)]
    place_y = [rows_of(s + 1, s + 2, rows) for s in (32, 40, 48)]
    spare = place_x + place_y
    for index, piece in enumerate((0, 0, 1, 1, 0, 2)):
        left[16 * index : 16 * index + 16, :] = jnp.concatenate([segment[piece], spare[index]], axis=0)
    levels = lax.broadcasted_iota(jnp.int32, (LAYERS, rows), 0).astype(F32)
    chosen = jnp.where(levels == rows_of(39, 40, rows), 1.0, 0.0)
    ones = jnp.ones((3, rows), F32)
    left[96:104, :] = chosen
    left[104:112, :] = chosen
    left[112:120, :] = chosen
    left[120:128, :] = jnp.concatenate([*squares(rows), ones, jnp.zeros((2, rows), F32)], axis=0)

    nets = rows_of(38, 39, cols)
    base = (rows_of(34, 37, cols) + rows_of(42, 45, cols) + rows_of(50, 53, cols)) * (SHIELD_FACTOR * scale)
    scaled = [groups(piece, nets) for piece in pieces(base)]
    blank = jnp.zeros((1, cols), F32)
    for index, piece in enumerate((0, 1, 0, 1, 2, 0)):
        right[16 * index : 16 * index + 16, :] = jnp.concatenate([scaled[piece], blank], axis=0).astype(BF16)
    right[96:128, :] = jnp.zeros((32, cols), BF16)
    coarse[0:96, :] = jnp.zeros((96, cols), BF16)
    levels = lax.broadcasted_iota(jnp.int32, (LAYERS, cols), 0).astype(F32)
    gap = levels * LAYER_PITCH - rows_of(39, 40, cols) * LAYER_PITCH
    ones = jnp.ones((3, cols), F32)
    coarse[96:128, :] = jnp.concatenate(
        [*pieces(gap * gap), ones, *squares(cols), jnp.zeros((2, cols), F32)], axis=0
    ).astype(BF16)
    own_x = rows_of(32, 33, cols) + rows_of(40, 41, cols) + rows_of(48, 49, cols)
    own_y = rows_of(33, 34, cols) + rows_of(41, 42, cols) + rows_of(49, 50, cols)
    line = lax.broadcasted_iota(jnp.int32, (128, 256), 0)
    lane = lax.broadcasted_iota(jnp.int32, (128, 256), 1)
    for_x = (lane < 128) & ((line == 15) | (line == 31) | (line == 47))
    for_y = (lane >= 128) & ((line == 63) | (line == 79) | (line == 95))
    xy[...] = jnp.where(for_x | for_y, 1.0, 0.0).astype(BF16)

    total[...] = jnp.zeros_like(total)

    def step(turn, carry):
        start = pl.multiple_of(turn * TILE_ROWS, TILE_ROWS)
        feats = left[:, pl.ds(start, TILE_ROWS)].T.astype(BF16)
        places = jnp.dot(feats, xy[...], preferred_element_type=F32)
        modes = stage[0:32, pl.ds(start, TILE_ROWS)].astype(BF16)
        tall_x = jnp.concatenate([places[:, 0:128]] * (TILE_COLS // 128), axis=1)
        tall_y = jnp.concatenate([places[:, 128:256]] * (TILE_COLS // 128), axis=1)
        for first in range(0, cols, TILE_COLS):
            here = slice(first, first + TILE_COLS)
            aligned = jnp.dot(feats, right[:, here], preferred_element_type=F32)
            spread = jnp.dot(feats, coarse[:, here], preferred_element_type=F32)
            delta_x = tall_x - own_x[:, here]
            delta_y = tall_y - own_y[:, here]
            spread = delta_x * delta_x + delta_y * delta_y + spread
            tile = (aligned * lax.rsqrt(spread)).astype(BF16)
            panel[pl.ds(start, TILE_ROWS), here] = tile
            total[:, here] += jnp.dot(modes, tile, preferred_element_type=F32)
        return carry

    lax.fori_loop(0, rows // TILE_ROWS, step, 0)
    centre = (low_edge[0] + high_edge[0]) * 0.5
    half_width = (high_edge[0] - low_edge[0]) * 0.5
    filtered[...] = ((total[...] - centre * stage[0:32, 0:cols]) / half_width).astype(BF16)


def product(panel, own, other):
    cols = own.shape[1]
    return jnp.dot(own[...], panel[0:cols, :], preferred_element_type=F32) + jnp.dot(
        other[...], panel[cols : 2 * cols, :], preferred_element_type=F32
    )


def second_body(panel, own, other, modes, low_edge, high_edge, second, second_low):
    count, _, width = modes.shape
    applied = product(panel, own, other)
    centre = (low_edge[0] + high_edge[0]) * 0.5
    half_width = (high_edge[0] - low_edge[0]) * 0.5
    second[...] = 2.0 * (applied - centre * own[...].astype(F32)) / half_width
    for place in range(count):
        here = slice(place * width, place * width + width)
        second[:, here] = second[:, here] - modes[place, 0:32, :].astype(F32)
    second_low[...] = second[...].astype(BF16)


def image_body(filaments, panel, own, other, second, sums):
    applied = product(panel, own, other)
    block = second[...]
    zeros = jnp.zeros_like(block)
    stacked = jnp.concatenate([block, zeros, applied, zeros], axis=0)
    sums[...] = (
        lax.dot_general(block, stacked, (((1,), (1,)), ((), ())), precision=HIGHEST, preferred_element_type=F32)
        / filaments
    )


def ritz_body(axes, sums, sums_other, second, ritz, projected):
    modes, width = ritz.shape
    line = lax.broadcasted_iota(jnp.int32, (modes, 128), 0)
    lane = lax.broadcasted_iota(jnp.int32, (modes, 128), 1)
    system = sums[...] + sums_other[...] + jnp.where(lane == line + modes, 1.0, 0.0)
    for pivot in range(modes):
        row = system[pivot : pivot + 1, :]
        column = system[:, pivot : pivot + 1] / system[pivot : pivot + 1, pivot : pivot + 1]
        column = jnp.where(line[:, 0:1] > pivot, column, 0.0)
        system = system - column * row
    diagonal = jnp.sum(jnp.where(lane == line, system, 0.0), axis=1, keepdims=True)
    system = system / jnp.sqrt(diagonal)
    inverse = system[:, modes : 2 * modes]
    half_solved = system[:, 2 * modes : 3 * modes]
    projected[...] = lax.dot_general(
        half_solved, inverse, (((1,), (1,)), ((), ())), precision=HIGHEST, preferred_element_type=F32
    )
    fil, col, col_size = axes
    place = lax.axis_index(fil) * (col_size // 2) + lax.axis_index(col) // 2
    if width % 128 == 0:
        mine = second[:, pl.ds(pl.multiple_of(place * width, 128), width)]
    else:
        odd = place % 2
        start = (place // 2) * (2 * width) + odd * (width - 64)
        window = second[:, pl.ds(pl.multiple_of(start, 128), width + 64)]
        moved = pltpu.roll(window, width, 1)
        mine = jnp.where(odd == 1, moved, window)[:, 0:width]
    ritz[...] = jnp.dot(inverse, mine, precision=HIGHEST, preferred_element_type=F32)


def call(body, name, out_shape, in_specs, scratch=(), limit=16):
    return pl.pallas_call(
        body,
        name=name,
        out_shape=out_shape,
        in_specs=in_specs,
        out_specs=jax.tree.map(lambda _: VMEM_SPEC, out_shape),
        scratch_shapes=list(scratch),
        compiler_params=pltpu.CompilerParams(vmem_limit_bytes=limit * 1024 * 1024),
    )


def paired_shards(geometry, net_ids, layers, trial_modes, low_edge, high_edge):
    width, modes = trial_modes.shape
    fil, col = lax.axis_size("fil"), lax.axis_size("col")
    count = fil * col // 2
    cols = count * width
    rows = 2 * cols
    shape = jax.ShapeDtypeStruct
    pair = [(i, i ^ 1) for i in range(col)]
    same_core = [[2 * chip + core for chip in range(count)] for core in range(2)]

    packed = call(pack_body, "pack", shape((count, PAYLOAD_ROWS, width), BF16), [VMEM_SPEC] * 4)(
        geometry, net_ids.reshape(1, width), layers.reshape(1, width), trial_modes.T
    )
    own = lax.all_to_all(packed, ("fil", "col"), 0, 0, axis_index_groups=same_core, tiled=True)
    other = lax.ppermute(own, "col", pair)
    panel, filtered = call(
        functools.partial(tile_body, 1.0 / math.sqrt(rows)),
        "tiles",
        (pltpu.VMEM((rows, cols), BF16), shape((modes, cols), BF16)),
        [VMEM_SPEC] * 2 + [SMEM_SPEC] * 2,
        [
            pltpu.VMEM((PAYLOAD_ROWS, rows), F32),
            pltpu.VMEM((128, rows), F32),
            pltpu.VMEM((128, cols), BF16),
            pltpu.VMEM((128, cols), BF16),
            pltpu.VMEM((128, 256), BF16),
            pltpu.VMEM((modes, cols), F32),
        ],
        limit=32,
    )(own, other, low_edge, high_edge)
    second, second_low = call(
        second_body,
        "second",
        (shape((modes, cols), F32), shape((modes, cols), BF16)),
        [VMEM_SPEC] * 4 + [SMEM_SPEC] * 2,
    )(panel, filtered, lax.ppermute(filtered, "col", pair), own, low_edge, high_edge)
    sums = call(functools.partial(image_body, float(rows)), "image", shape((modes, 128), F32), [VMEM_SPEC] * 4)(
        panel, second_low, lax.ppermute(second_low, "col", pair), second
    )
    ritz, projected = call(
        functools.partial(ritz_body, ("fil", "col", col)),
        "ritz",
        (shape((modes, width), F32), shape((modes, modes), F32)),
        [VMEM_SPEC] * 3,
    )(sums, lax.ppermute(sums, "col", pair), second)
    return ritz.T, projected


def features(geometry, net_ids, layers):
    height = layers.astype(F32) * LAYER_PITCH
    return jnp.concatenate([geometry[0:2], height[None], geometry[2:6], net_ids.astype(F32)[None]], axis=0)


def kernel_tile(row_feat, col_feat, kernel_scale):
    delta_x = row_feat[0][:, None] - col_feat[0][None, :]
    delta_y = row_feat[1][:, None] - col_feat[1][None, :]
    delta_z = row_feat[2][:, None] - col_feat[2][None, :]
    radius_sq = (
        row_feat[6][:, None] * row_feat[6][:, None] + col_feat[6][None, :] * col_feat[6][None, :]
    )
    spread = delta_x * delta_x + delta_y * delta_y + delta_z * delta_z + radius_sq
    alignment = (
        row_feat[3][:, None] * col_feat[3][None, :]
        + row_feat[4][:, None] * col_feat[4][None, :]
        + row_feat[5][:, None] * col_feat[5][None, :]
    )
    couple = jnp.where(row_feat[7][:, None] == col_feat[7][None, :], 1.0, SHIELD_FACTOR)
    return (alignment * couple * lax.rsqrt(spread) * kernel_scale).astype(BF16)


def column_span(length, tile_rows, shard_rows):
    span_limit = max(shard_rows, (1 << 20) // tile_rows)
    span_cols = shard_rows
    while span_cols * 2 <= span_limit and length % (span_cols * 2) == 0:
        span_cols = span_cols * 2
    return span_cols


def accumulate(running, row_feat, part_feats, gathered, kernel_scale, span_cols):
    turns = gathered.shape[0] // span_cols

    def one_span(turn_index, partial_sum):
        offset = turn_index * span_cols
        span_feats = lax.dynamic_slice_in_dim(part_feats, offset, span_cols, 1)
        span_modes = lax.dynamic_slice_in_dim(gathered, offset, span_cols, 0)
        tile_vals = kernel_tile(row_feat, span_feats, kernel_scale)
        return partial_sum + jnp.dot(tile_vals, span_modes, preferred_element_type=F32)

    return lax.fori_loop(0, turns, one_span, running)


def general_shards(geometry, net_ids, layers, trial_modes, low_edge, high_edge):
    own_rows, modes_count = trial_modes.shape
    filaments = own_rows * lax.axis_size("fil") * lax.axis_size("col")
    kernel_scale = 1.0 / math.sqrt(filaments)
    own_feats = features(geometry, net_ids, layers)
    row_feat = lax.all_gather(own_feats, "col", axis=1, tiled=True)
    col_feat = lax.all_gather(own_feats, "fil", axis=1, tiled=True)
    tile_rows = row_feat.shape[1]

    def apply_operator(mode_block):
        gathered = lax.all_gather(mode_block, "fil", axis=0, tiled=True)
        initial = jnp.zeros((tile_rows, modes_count), F32)
        span = column_span(gathered.shape[0], tile_rows, own_rows)
        partial_value = accumulate(initial, row_feat, col_feat, gathered, kernel_scale, span)
        summed = lax.psum(partial_value, "col")
        return lax.dynamic_slice_in_dim(summed, lax.axis_index("col") * own_rows, own_rows, 0)

    centre = (low_edge[0] + high_edge[0]) * 0.5
    half_width = (high_edge[0] - low_edge[0]) * 0.5
    filtered_one = (
        (apply_operator(trial_modes) - centre * trial_modes.astype(F32)) / half_width
    ).astype(BF16)
    second = 2.0 * (
        apply_operator(filtered_one) - centre * filtered_one.astype(F32)
    ) / half_width - trial_modes.astype(F32)
    second_low = second.astype(BF16)
    gram_local = jnp.dot(second.T, second, precision=HIGHEST) / filaments
    image_block = apply_operator(second_low)
    cross_local = jnp.dot(second.T, image_block, precision=HIGHEST) / filaments
    gram_matrix, cross_matrix = lax.psum((gram_local, cross_local), ("fil", "col"))
    factor = jnp.linalg.cholesky(gram_matrix)
    ritz_basis = jax.scipy.linalg.solve_triangular(factor, second.T, lower=True).T
    half_solved = jax.scipy.linalg.solve_triangular(factor, cross_matrix, lower=True)
    projected = jax.scipy.linalg.solve_triangular(factor, half_solved.T, lower=True).T
    return (ritz_basis, projected)


def fits(mesh, width, modes):
    count = mesh.shape["fil"] * mesh.shape["col"]
    rows = count * width
    return (
        mesh.shape["col"] % 2 == 0
        and (count // 2) % 2 == 0
        and modes == 32
        and width % 64 == 0
        and (rows // 2) % TILE_COLS == 0
        and rows % TILE_ROWS == 0
        and rows * rows <= 16 * 1024 * 1024
    )


def solution(mesh):
    in_specs = (
        P(None, ("groups", "fil", "col")),
        P(("groups", "fil", "col")),
        P(("groups", "fil", "col")),
        P(("groups", "fil", "col"), None),
        P("groups"),
        P("groups"),
    )
    out_specs = (P(("groups", "fil", "col"), None), P("groups", None))

    def shards(geometry, net_ids, layers, trial_modes, low_edge, high_edge):
        form = paired_shards if fits(mesh, *trial_modes.shape) else general_shards
        return form(geometry, net_ids, layers, trial_modes, low_edge, high_edge)

    return jax.shard_map(shards, mesh=mesh, in_specs=in_specs, out_specs=out_specs, check_vma=False)
```

```python
import functools
import math

import jax
import jax.numpy as jnp
from jax import lax
from jax.experimental import pallas as pl
from jax.experimental.pallas import tpu as pltpu
from jax.sharding import PartitionSpec as P

SHIELD_FACTOR = 0.5
LAYER_PITCH = 0.02
NETS = 4
LAYERS = 8
F32 = jnp.float32
BF16 = jnp.bfloat16
HIGHEST = lax.Precision.HIGHEST
VMEM_SPEC = pl.BlockSpec(memory_space=pltpu.VMEM)
SMEM_SPEC = pl.BlockSpec(memory_space=pltpu.SMEM)
PAYLOAD_ROWS = 64
TILE_ROWS = 512
TILE_COLS = 256


def pieces(x):
    high = x.astype(BF16).astype(F32)
    mid = (x - high).astype(BF16).astype(F32)
    low = (x - high - mid).astype(BF16).astype(F32)
    return high, mid, low


def pack_body(geometry, nets, layers, modes, out):
    shape = (1, geometry.shape[1])
    high, mid, low = pieces(geometry[...])
    zeros = jnp.zeros((2,) + shape[1:], F32)
    rest = jnp.zeros((8,) + shape[1:], F32)
    rows = jnp.concatenate(
        [high, nets[...].astype(F32), layers[...].astype(F32), mid, zeros, low, zeros, rest], axis=0
    ).astype(BF16)
    for place in range(out.shape[0]):
        out[place, 0:32, :] = modes[...]
        out[place, 32:64, :] = rows


def tile_body(scale, own, other, low_edge, high_edge, panel_own, panel_other, filtered, stage, left, right, coarse, xy, total):
    count, _, width = own.shape
    cols = count * width
    rows = 2 * cols
    panels = (panel_own, panel_other)
    for half, part in enumerate((own, other)):
        for place in range(count):
            start = half * cols + place * width
            stage[:, start : start + width] = part[place].astype(F32)

    def rows_of(first, last, length):
        return stage[first:last, 0:length]

    def groups(base, nets):
        listed = [base] + [jnp.where(nets == float(n), base, 0.0) for n in range(NETS)]
        return jnp.concatenate(listed, axis=0)

    def squares(length):
        return pieces(jnp.square(rows_of(37, 38, length) + rows_of(45, 46, length) + rows_of(53, 54, length)))

    nets = rows_of(38, 39, rows)
    segment = [groups(rows_of(s + 2, s + 5, rows), nets) for s in (32, 40, 48)]
    place_x = [rows_of(s, s + 1, rows) for s in (32, 40, 48)]
    place_y = [rows_of(s + 1, s + 2, rows) for s in (32, 40, 48)]
    spare = place_x + place_y
    for index, piece in enumerate((0, 0, 1, 1, 0, 2)):
        left[16 * index : 16 * index + 16, :] = jnp.concatenate([segment[piece], spare[index]], axis=0)
    levels = lax.broadcasted_iota(jnp.int32, (LAYERS, rows), 0).astype(F32)
    chosen = jnp.where(levels == rows_of(39, 40, rows), 1.0, 0.0)
    ones = jnp.ones((3, rows), F32)
    left[96:104, :] = chosen
    left[104:112, :] = chosen
    left[112:120, :] = chosen
    left[120:128, :] = jnp.concatenate([*squares(rows), ones, jnp.zeros((2, rows), F32)], axis=0)

    nets = rows_of(38, 39, cols)
    base = (rows_of(34, 37, cols) + rows_of(42, 45, cols) + rows_of(50, 53, cols)) * (SHIELD_FACTOR * scale)
    scaled = [groups(piece, nets) for piece in pieces(base)]
    blank = jnp.zeros((1, cols), F32)
    for index, piece in enumerate((0, 1, 0, 1, 2, 0)):
        right[16 * index : 16 * index + 16, :] = jnp.concatenate([scaled[piece], blank], axis=0).astype(BF16)
    right[96:128, :] = jnp.zeros((32, cols), BF16)
    coarse[0:96, :] = jnp.zeros((96, cols), BF16)
    levels = lax.broadcasted_iota(jnp.int32, (LAYERS, cols), 0).astype(F32)
    gap = levels * LAYER_PITCH - rows_of(39, 40, cols) * LAYER_PITCH
    ones = jnp.ones((3, cols), F32)
    coarse[96:128, :] = jnp.concatenate(
        [*pieces(gap * gap), ones, *squares(cols), jnp.zeros((2, cols), F32)], axis=0
    ).astype(BF16)
    own_x = rows_of(32, 33, cols) + rows_of(40, 41, cols) + rows_of(48, 49, cols)
    own_y = rows_of(33, 34, cols) + rows_of(41, 42, cols) + rows_of(49, 50, cols)
    line = lax.broadcasted_iota(jnp.int32, (128, 256), 0)
    lane = lax.broadcasted_iota(jnp.int32, (128, 256), 1)
    for_x = (lane < 128) & ((line == 15) | (line == 31) | (line == 47))
    for_y = (lane >= 128) & ((line == 63) | (line == 79) | (line == 95))
    xy[...] = jnp.where(for_x | for_y, 1.0, 0.0).astype(BF16)

    total[...] = jnp.zeros_like(total)

    def generate(half, turn):
        near = pl.multiple_of(turn * TILE_ROWS, TILE_ROWS)
        start = pl.multiple_of(half * cols + turn * TILE_ROWS, TILE_ROWS)
        panel = panels[half]
        feats = left[:, pl.ds(start, TILE_ROWS)].T.astype(BF16)
        places = jnp.dot(feats, xy[...], preferred_element_type=F32)
        tall_x = jnp.concatenate([places[:, 0:128]] * (TILE_COLS // 128), axis=1)
        tall_y = jnp.concatenate([places[:, 128:256]] * (TILE_COLS // 128), axis=1)
        for first in range(0, cols, TILE_COLS):
            here = slice(first, first + TILE_COLS)
            aligned = jnp.dot(feats, right[:, here], preferred_element_type=F32)
            spread = jnp.dot(feats, coarse[:, here], preferred_element_type=F32)
            delta_x = tall_x - own_x[:, here]
            delta_y = tall_y - own_y[:, here]
            spread = delta_x * delta_x + delta_y * delta_y + spread
            panel[pl.ds(near, TILE_ROWS), here] = (aligned * lax.rsqrt(spread)).astype(BF16)

    def multiply(half, turn):
        near = pl.multiple_of(turn * TILE_ROWS, TILE_ROWS)
        start = pl.multiple_of(half * cols + turn * TILE_ROWS, TILE_ROWS)
        modes = stage[0:32, pl.ds(start, TILE_ROWS)].astype(BF16)
        total[...] += jnp.dot(modes, panels[half][pl.ds(near, TILE_ROWS), :], preferred_element_type=F32)

    generate(0, 0)

    def step(turn, carry):
        multiply(0, turn)
        generate(1, turn)
        multiply(1, turn)
        generate(0, turn + 1)
        return carry

    last = cols // TILE_ROWS - 1
    lax.fori_loop(0, last, step, 0)
    multiply(0, last)
    generate(1, last)
    multiply(1, last)
    centre = (low_edge[0] + high_edge[0]) * 0.5
    half_width = (high_edge[0] - low_edge[0]) * 0.5
    filtered[...] = ((total[...] - centre * stage[0:32, 0:cols]) / half_width).astype(BF16)


def product(panel_own, panel_other, own, other):
    return jnp.dot(own[...], panel_own[...], preferred_element_type=F32) + jnp.dot(
        other[...], panel_other[...], preferred_element_type=F32
    )


def second_body(panel_own, panel_other, own, other, modes, low_edge, high_edge, second, second_low):
    count, _, width = modes.shape
    applied = product(panel_own, panel_other, own, other)
    centre = (low_edge[0] + high_edge[0]) * 0.5
    half_width = (high_edge[0] - low_edge[0]) * 0.5
    second[...] = 2.0 * (applied - centre * own[...].astype(F32)) / half_width
    for place in range(count):
        here = slice(place * width, place * width + width)
        second[:, here] = second[:, here] - modes[place, 0:32, :].astype(F32)
    second_low[...] = second[...].astype(BF16)


def image_body(filaments, panel_own, panel_other, own, other, second, sums):
    applied = product(panel_own, panel_other, own, other)
    block = second[...]
    zeros = jnp.zeros_like(block)
    stacked = jnp.concatenate([block, zeros, applied, zeros], axis=0)
    sums[...] = (
        lax.dot_general(block, stacked, (((1,), (1,)), ((), ())), precision=HIGHEST, preferred_element_type=F32)
        / filaments
    )


def ritz_body(axes, sums, sums_other, second, ritz, projected):
    modes, width = ritz.shape
    line = lax.broadcasted_iota(jnp.int32, (modes, 128), 0)
    lane = lax.broadcasted_iota(jnp.int32, (modes, 128), 1)
    system = sums[...] + sums_other[...] + jnp.where(lane == line + modes, 1.0, 0.0)
    for pivot in range(modes):
        row = system[pivot : pivot + 1, :]
        column = system[:, pivot : pivot + 1] / system[pivot : pivot + 1, pivot : pivot + 1]
        column = jnp.where(line[:, 0:1] > pivot, column, 0.0)
        system = system - column * row
    diagonal = jnp.sum(jnp.where(lane == line, system, 0.0), axis=1, keepdims=True)
    system = system / jnp.sqrt(diagonal)
    inverse = system[:, modes : 2 * modes]
    half_solved = system[:, 2 * modes : 3 * modes]
    projected[...] = lax.dot_general(
        half_solved, inverse, (((1,), (1,)), ((), ())), precision=HIGHEST, preferred_element_type=F32
    )
    fil, col, col_size = axes
    place = lax.axis_index(fil) * (col_size // 2) + lax.axis_index(col) // 2
    if width % 128 == 0:
        mine = second[:, pl.ds(pl.multiple_of(place * width, 128), width)]
    else:
        odd = place % 2
        start = (place // 2) * (2 * width) + odd * (width - 64)
        window = second[:, pl.ds(pl.multiple_of(start, 128), width + 64)]
        moved = pltpu.roll(window, width, 1)
        mine = jnp.where(odd == 1, moved, window)[:, 0:width]
    ritz[...] = jnp.dot(inverse, mine, precision=HIGHEST, preferred_element_type=F32)


def call(body, name, out_shape, in_specs, scratch=(), limit=16):
    return pl.pallas_call(
        body,
        name=name,
        out_shape=out_shape,
        in_specs=in_specs,
        out_specs=jax.tree.map(lambda _: VMEM_SPEC, out_shape),
        scratch_shapes=list(scratch),
        compiler_params=pltpu.CompilerParams(vmem_limit_bytes=limit * 1024 * 1024),
    )


def paired_shards(geometry, net_ids, layers, trial_modes, low_edge, high_edge):
    width, modes = trial_modes.shape
    fil, col = lax.axis_size("fil"), lax.axis_size("col")
    count = fil * col // 2
    cols = count * width
    rows = 2 * cols
    shape = jax.ShapeDtypeStruct
    pair = [(i, i ^ 1) for i in range(col)]
    same_core = [[2 * chip + core for chip in range(count)] for core in range(2)]

    packed = call(pack_body, "pack", shape((count, PAYLOAD_ROWS, width), BF16), [VMEM_SPEC] * 4)(
        geometry, net_ids.reshape(1, width), layers.reshape(1, width), trial_modes.T
    )
    own = lax.all_to_all(packed, ("fil", "col"), 0, 0, axis_index_groups=same_core, tiled=True)
    other = lax.ppermute(own, "col", pair)
    panel_own, panel_other, filtered = call(
        functools.partial(tile_body, 1.0 / math.sqrt(rows)),
        "tiles",
        (pltpu.VMEM((cols, cols), BF16), pltpu.VMEM((cols, cols), BF16), shape((modes, cols), BF16)),
        [VMEM_SPEC] * 2 + [SMEM_SPEC] * 2,
        [
            pltpu.VMEM((PAYLOAD_ROWS, rows), F32),
            pltpu.VMEM((128, rows), F32),
            pltpu.VMEM((128, cols), BF16),
            pltpu.VMEM((128, cols), BF16),
            pltpu.VMEM((128, 256), BF16),
            pltpu.VMEM((modes, cols), F32),
        ],
        limit=32,
    )(own, other, low_edge, high_edge)
    second, second_low = call(
        second_body,
        "second",
        (shape((modes, cols), F32), shape((modes, cols), BF16)),
        [VMEM_SPEC] * 5 + [SMEM_SPEC] * 2,
    )(panel_own, panel_other, filtered, lax.ppermute(filtered, "col", pair), own, low_edge, high_edge)
    sums = call(functools.partial(image_body, float(rows)), "image", shape((modes, 128), F32), [VMEM_SPEC] * 5)(
        panel_own, panel_other, second_low, lax.ppermute(second_low, "col", pair), second
    )
    ritz, projected = call(
        functools.partial(ritz_body, ("fil", "col", col)),
        "ritz",
        (shape((modes, width), F32), shape((modes, modes), F32)),
        [VMEM_SPEC] * 3,
    )(sums, lax.ppermute(sums, "col", pair), second)
    return ritz.T, projected


def features(geometry, net_ids, layers):
    height = layers.astype(F32) * LAYER_PITCH
    return jnp.concatenate([geometry[0:2], height[None], geometry[2:6], net_ids.astype(F32)[None]], axis=0)


def kernel_tile(row_feat, col_feat, kernel_scale):
    delta_x = row_feat[0][:, None] - col_feat[0][None, :]
    delta_y = row_feat[1][:, None] - col_feat[1][None, :]
    delta_z = row_feat[2][:, None] - col_feat[2][None, :]
    radius_sq = (
        row_feat[6][:, None] * row_feat[6][:, None] + col_feat[6][None, :] * col_feat[6][None, :]
    )
    spread = delta_x * delta_x + delta_y * delta_y + delta_z * delta_z + radius_sq
    alignment = (
        row_feat[3][:, None] * col_feat[3][None, :]
        + row_feat[4][:, None] * col_feat[4][None, :]
        + row_feat[5][:, None] * col_feat[5][None, :]
    )
    couple = jnp.where(row_feat[7][:, None] == col_feat[7][None, :], 1.0, SHIELD_FACTOR)
    return (alignment * couple * lax.rsqrt(spread) * kernel_scale).astype(BF16)


def column_span(length, tile_rows, shard_rows):
    span_limit = max(shard_rows, (1 << 20) // tile_rows)
    span_cols = shard_rows
    while span_cols * 2 <= span_limit and length % (span_cols * 2) == 0:
        span_cols = span_cols * 2
    return span_cols


def accumulate(running, row_feat, part_feats, gathered, kernel_scale, span_cols):
    turns = gathered.shape[0] // span_cols

    def one_span(turn_index, partial_sum):
        offset = turn_index * span_cols
        span_feats = lax.dynamic_slice_in_dim(part_feats, offset, span_cols, 1)
        span_modes = lax.dynamic_slice_in_dim(gathered, offset, span_cols, 0)
        tile_vals = kernel_tile(row_feat, span_feats, kernel_scale)
        return partial_sum + jnp.dot(tile_vals, span_modes, preferred_element_type=F32)

    return lax.fori_loop(0, turns, one_span, running)


def general_shards(geometry, net_ids, layers, trial_modes, low_edge, high_edge):
    own_rows, modes_count = trial_modes.shape
    filaments = own_rows * lax.axis_size("fil") * lax.axis_size("col")
    kernel_scale = 1.0 / math.sqrt(filaments)
    own_feats = features(geometry, net_ids, layers)
    row_feat = lax.all_gather(own_feats, "col", axis=1, tiled=True)
    col_feat = lax.all_gather(own_feats, "fil", axis=1, tiled=True)
    tile_rows = row_feat.shape[1]

    def apply_operator(mode_block):
        gathered = lax.all_gather(mode_block, "fil", axis=0, tiled=True)
        initial = jnp.zeros((tile_rows, modes_count), F32)
        span = column_span(gathered.shape[0], tile_rows, own_rows)
        partial_value = accumulate(initial, row_feat, col_feat, gathered, kernel_scale, span)
        summed = lax.psum(partial_value, "col")
        return lax.dynamic_slice_in_dim(summed, lax.axis_index("col") * own_rows, own_rows, 0)

    centre = (low_edge[0] + high_edge[0]) * 0.5
    half_width = (high_edge[0] - low_edge[0]) * 0.5
    filtered_one = (
        (apply_operator(trial_modes) - centre * trial_modes.astype(F32)) / half_width
    ).astype(BF16)
    second = 2.0 * (
        apply_operator(filtered_one) - centre * filtered_one.astype(F32)
    ) / half_width - trial_modes.astype(F32)
    second_low = second.astype(BF16)
    gram_local = jnp.dot(second.T, second, precision=HIGHEST) / filaments
    image_block = apply_operator(second_low)
    cross_local = jnp.dot(second.T, image_block, precision=HIGHEST) / filaments
    gram_matrix, cross_matrix = lax.psum((gram_local, cross_local), ("fil", "col"))
    factor = jnp.linalg.cholesky(gram_matrix)
    ritz_basis = jax.scipy.linalg.solve_triangular(factor, second.T, lower=True).T
    half_solved = jax.scipy.linalg.solve_triangular(factor, cross_matrix, lower=True)
    projected = jax.scipy.linalg.solve_triangular(factor, half_solved.T, lower=True).T
    return (ritz_basis, projected)


def fits(mesh, width, modes):
    count = mesh.shape["fil"] * mesh.shape["col"]
    rows = count * width
    return (
        mesh.shape["col"] % 2 == 0
        and (count // 2) % 2 == 0
        and modes == 32
        and width % 64 == 0
        and (rows // 2) % TILE_COLS == 0
        and (rows // 2) % TILE_ROWS == 0
        and rows * rows <= 16 * 1024 * 1024
    )


def solution(mesh):
    in_specs = (
        P(None, ("groups", "fil", "col")),
        P(("groups", "fil", "col")),
        P(("groups", "fil", "col")),
        P(("groups", "fil", "col"), None),
        P("groups"),
        P("groups"),
    )
    out_specs = (P(("groups", "fil", "col"), None), P("groups", None))

    def shards(geometry, net_ids, layers, trial_modes, low_edge, high_edge):
        form = paired_shards if fits(mesh, *trial_modes.shape) else general_shards
        return form(geometry, net_ids, layers, trial_modes, low_edge, high_edge)

    return jax.shard_map(shards, mesh=mesh, in_specs=in_specs, out_specs=out_specs, check_vma=False)
```

```python
import functools
import math

import jax
import jax.numpy as jnp
from jax import lax
from jax.experimental import pallas as pl
from jax.experimental.pallas import tpu as pltpu
from jax.sharding import PartitionSpec as P

SHIELD_FACTOR = 0.5
LAYER_PITCH = 0.02
NETS = 4
LAYERS = 8
F32 = jnp.float32
BF16 = jnp.bfloat16
HIGHEST = lax.Precision.HIGHEST
VMEM_SPEC = pl.BlockSpec(memory_space=pltpu.VMEM)
WIDTH = 192
TILE_ROWS = 512
TILE_COLS = 256


def pieces(x):
    high = x.astype(BF16).astype(F32)
    mid = (x - high).astype(BF16).astype(F32)
    low = (x - high - mid).astype(BF16).astype(F32)
    return high, mid, low


def pack_body(geometry, nets, layers, modes, out, *scratch):
    copies = []
    for index, source in enumerate((geometry, nets, layers, modes)):
        copies.append(pltpu.make_async_copy(source, scratch[index], scratch[4].at[index]))
        copies[-1].start()
    for copy in copies:
        copy.wait()
    geometry, nets, layers, modes, _, sheet = scratch
    high, mid, low = pieces(geometry[...])
    zeros = jnp.zeros((2, WIDTH), F32)
    rows = jnp.concatenate(
        [high, nets[...].astype(F32), layers[...].astype(F32), mid, zeros, low, zeros], axis=0
    )
    sheet[...] = jnp.zeros_like(sheet)
    sheet[0:32, 0:WIDTH] = modes[...].astype(F32)
    sheet[0:24, 192:256] = rows[:, 0:64]
    sheet[32:48, 0:64] = rows[0:16, 64:128]
    sheet[32:40, 64:128] = rows[16:24, 64:128]
    sheet[40:48, 64:128] = rows[0:8, 128:192]
    sheet[32:48, 128:192] = rows[8:24, 128:192]
    packed = sheet[...].astype(BF16)
    for place in range(out.shape[0]):
        out[place] = packed


def unpack(part, stage, half):
    for place in range(part.shape[0]):
        start = (half * part.shape[0] + place) * WIDTH
        sheet = part[place].astype(F32)
        stage[0:32, start : start + WIDTH] = sheet[0:32, 0:WIDTH]
        stage[32:56, start : start + 64] = sheet[0:24, 192:256]
        stage[32:48, start + 64 : start + 128] = sheet[32:48, 0:64]
        stage[48:56, start + 64 : start + 128] = sheet[32:40, 64:128]
        stage[32:40, start + 128 : start + 192] = sheet[40:48, 64:128]
        stage[40:56, start + 128 : start + 192] = sheet[32:48, 128:192]


def tile_body(scale, own, other, edges, panel_own, panel_other, filtered, stage, left, right, coarse, xy, total):
    cols = own.shape[0] * WIDTH
    rows = 2 * cols
    panels = (panel_own, panel_other)
    unpack(own, stage, 0)
    unpack(other, stage, 1)

    def rows_of(first, last, length):
        return stage[first:last, 0:length]

    def groups(base, nets):
        listed = [base] + [jnp.where(nets == float(n), base, 0.0) for n in range(NETS)]
        return jnp.concatenate(listed, axis=0)

    def squares(length):
        return pieces(jnp.square(rows_of(37, 38, length) + rows_of(45, 46, length) + rows_of(53, 54, length)))

    nets = rows_of(38, 39, rows)
    segment = [groups(rows_of(s + 2, s + 5, rows), nets) for s in (32, 40, 48)]
    place_x = [rows_of(s, s + 1, rows) for s in (32, 40, 48)]
    place_y = [rows_of(s + 1, s + 2, rows) for s in (32, 40, 48)]
    spare = place_x + place_y
    for index, piece in enumerate((0, 0, 1, 1, 0, 2)):
        left[16 * index : 16 * index + 16, :] = jnp.concatenate([segment[piece], spare[index]], axis=0)
    levels = lax.broadcasted_iota(jnp.int32, (LAYERS, rows), 0).astype(F32)
    chosen = jnp.where(levels == rows_of(39, 40, rows), 1.0, 0.0)
    ones = jnp.ones((3, rows), F32)
    left[96:104, :] = chosen
    left[104:112, :] = chosen
    left[112:120, :] = chosen
    left[120:128, :] = jnp.concatenate([*squares(rows), ones, jnp.zeros((2, rows), F32)], axis=0)

    nets = rows_of(38, 39, cols)
    base = (rows_of(34, 37, cols) + rows_of(42, 45, cols) + rows_of(50, 53, cols)) * (SHIELD_FACTOR * scale)
    scaled = [groups(piece, nets) for piece in pieces(base)]
    blank = jnp.zeros((1, cols), F32)
    for index, piece in enumerate((0, 1, 0, 1, 2, 0)):
        right[16 * index : 16 * index + 16, :] = jnp.concatenate([scaled[piece], blank], axis=0).astype(BF16)
    right[96:128, :] = jnp.zeros((32, cols), BF16)
    coarse[0:96, :] = jnp.zeros((96, cols), BF16)
    levels = lax.broadcasted_iota(jnp.int32, (LAYERS, cols), 0).astype(F32)
    gap = levels * LAYER_PITCH - rows_of(39, 40, cols) * LAYER_PITCH
    ones = jnp.ones((3, cols), F32)
    coarse[96:128, :] = jnp.concatenate(
        [*pieces(gap * gap), ones, *squares(cols), jnp.zeros((2, cols), F32)], axis=0
    ).astype(BF16)
    own_x = rows_of(32, 33, cols) + rows_of(40, 41, cols) + rows_of(48, 49, cols)
    own_y = rows_of(33, 34, cols) + rows_of(41, 42, cols) + rows_of(49, 50, cols)
    line = lax.broadcasted_iota(jnp.int32, (128, 256), 0)
    lane = lax.broadcasted_iota(jnp.int32, (128, 256), 1)
    for_x = (lane < 128) & ((line == 15) | (line == 31) | (line == 47))
    for_y = (lane >= 128) & ((line == 63) | (line == 79) | (line == 95))
    xy[...] = jnp.where(for_x | for_y, 1.0, 0.0).astype(BF16)

    total[...] = jnp.zeros_like(total)

    def generate(half, turn):
        near = pl.multiple_of(turn * TILE_ROWS, TILE_ROWS)
        start = pl.multiple_of(half * cols + turn * TILE_ROWS, TILE_ROWS)
        panel = panels[half]
        feats = left[:, pl.ds(start, TILE_ROWS)].T.astype(BF16)
        places = jnp.dot(feats, xy[...], preferred_element_type=F32)
        tall_x = jnp.concatenate([places[:, 0:128]] * (TILE_COLS // 128), axis=1)
        tall_y = jnp.concatenate([places[:, 128:256]] * (TILE_COLS // 128), axis=1)
        for first in range(0, cols, TILE_COLS):
            here = slice(first, first + TILE_COLS)
            aligned = jnp.dot(feats, right[:, here], preferred_element_type=F32)
            spread = jnp.dot(feats, coarse[:, here], preferred_element_type=F32)
            delta_x = tall_x - own_x[:, here]
            delta_y = tall_y - own_y[:, here]
            spread = delta_x * delta_x + delta_y * delta_y + spread
            panel[pl.ds(near, TILE_ROWS), here] = (aligned * lax.rsqrt(spread)).astype(BF16)

    def multiply(half, turn):
        near = pl.multiple_of(turn * TILE_ROWS, TILE_ROWS)
        start = pl.multiple_of(half * cols + turn * TILE_ROWS, TILE_ROWS)
        modes = stage[0:32, pl.ds(start, TILE_ROWS)].astype(BF16)
        total[...] += jnp.dot(modes, panels[half][pl.ds(near, TILE_ROWS), :], preferred_element_type=F32)

    generate(0, 0)

    def step(turn, carry):
        multiply(0, turn)
        generate(1, turn)
        multiply(1, turn)
        generate(0, turn + 1)
        return carry

    last = cols // TILE_ROWS - 1
    lax.fori_loop(0, last, step, 0)
    multiply(0, last)
    generate(1, last)
    multiply(1, last)
    centre, half_width = edges[0:1, 0:1], edges[1:2, 0:1]
    filtered[...] = ((total[...] - centre * stage[0:32, 0:cols]) / half_width).astype(BF16)


def product(panel_own, panel_other, own, other):
    return jnp.dot(own[...], panel_own[...], preferred_element_type=F32) + jnp.dot(
        other[...], panel_other[...], preferred_element_type=F32
    )


def second_body(panel_own, panel_other, own, other, modes, edges, second, second_low):
    count = modes.shape[0]
    applied = product(panel_own, panel_other, own, other)
    centre, half_width = edges[0:1, 0:1], edges[1:2, 0:1]
    second[...] = 2.0 * (applied - centre * own[...].astype(F32)) / half_width
    for place in range(count):
        here = slice(place * WIDTH, place * WIDTH + WIDTH)
        second[:, here] = second[:, here] - modes[place, 0:32, 0:WIDTH].astype(F32)
    second_low[...] = second[...].astype(BF16)


def image_body(filaments, panel_own, panel_other, own, other, second, sums):
    applied = product(panel_own, panel_other, own, other)
    block = second[...]
    zeros = jnp.zeros_like(block)
    stacked = jnp.concatenate([block, zeros, applied, zeros], axis=0)
    sums[...] = (
        lax.dot_general(block, stacked, (((1,), (1,)), ((), ())), precision=HIGHEST, preferred_element_type=F32)
        / filaments
    )


def ritz_body(axes, sums, sums_other, second, ritz, projected):
    modes, width = ritz.shape
    line = lax.broadcasted_iota(jnp.int32, (modes, 128), 0)
    lane = lax.broadcasted_iota(jnp.int32, (modes, 128), 1)
    system = sums[...] + sums_other[...] + jnp.where(lane == line + modes, 1.0, 0.0)
    for pivot in range(modes):
        row = system[pivot : pivot + 1, :]
        column = system[:, pivot : pivot + 1] / system[pivot : pivot + 1, pivot : pivot + 1]
        column = jnp.where(line[:, 0:1] > pivot, column, 0.0)
        system = system - column * row
    diagonal = jnp.sum(jnp.where(lane == line, system, 0.0), axis=1, keepdims=True)
    system = system / jnp.sqrt(diagonal)
    inverse = system[:, modes : 2 * modes]
    half_solved = system[:, 2 * modes : 3 * modes]
    projected[...] = lax.dot_general(
        half_solved, inverse, (((1,), (1,)), ((), ())), precision=HIGHEST, preferred_element_type=F32
    )
    fil, col, col_size = axes
    place = lax.axis_index(fil) * (col_size // 2) + lax.axis_index(col) // 2
    if width % 128 == 0:
        mine = second[:, pl.ds(pl.multiple_of(place * width, 128), width)]
    else:
        odd = place % 2
        start = (place // 2) * (2 * width) + odd * (width - 64)
        window = second[:, pl.ds(pl.multiple_of(start, 128), width + 64)]
        moved = pltpu.roll(window, width, 1)
        mine = jnp.where(odd == 1, moved, window)[:, 0:width]
    ritz[...] = jnp.dot(inverse, mine, precision=HIGHEST, preferred_element_type=F32)


def call(body, name, out_shape, in_specs, scratch=(), limit=16):
    return pl.pallas_call(
        body,
        name=name,
        out_shape=out_shape,
        in_specs=in_specs,
        out_specs=jax.tree.map(lambda _: VMEM_SPEC, out_shape),
        scratch_shapes=list(scratch),
        compiler_params=pltpu.CompilerParams(vmem_limit_bytes=limit * 1024 * 1024),
    )


def paired_shards(geometry, net_ids, layers, trial_modes, low_edge, high_edge):
    width, modes = trial_modes.shape
    fil, col = lax.axis_size("fil"), lax.axis_size("col")
    count = fil * col // 2
    cols = count * width
    rows = 2 * cols
    shape = jax.ShapeDtypeStruct
    pair = [(i, i ^ 1) for i in range(col)]
    same_core = [[2 * chip + core for chip in range(count)] for core in range(2)]

    packed = call(
        pack_body,
        "pack",
        shape((count, 48, 256), BF16),
        [pl.BlockSpec(memory_space=pl.ANY)] * 4,
        [
            pltpu.VMEM(geometry.shape, F32),
            pltpu.VMEM((1, width), jnp.int32),
            pltpu.VMEM((1, width), jnp.int32),
            pltpu.VMEM((modes, width), BF16),
            pltpu.SemaphoreType.DMA((4,)),
            pltpu.VMEM((48, 256), F32),
        ],
    )(
        *(
            pltpu.with_memory_space_constraint(x, pltpu.HBM)
            for x in (
                geometry,
                net_ids.reshape(1, width),
                layers.reshape(1, width),
                trial_modes.T,
            )
        )
    )
    ends = jnp.stack([(low_edge + high_edge) * 0.5, (high_edge - low_edge) * 0.5])
    edges = jnp.broadcast_to(ends, (2, 128))
    own = lax.all_to_all(packed, ("fil", "col"), 0, 0, axis_index_groups=same_core, tiled=True)
    other = lax.ppermute(own, "col", pair)
    panel_own, panel_other, filtered = call(
        functools.partial(tile_body, 1.0 / math.sqrt(rows)),
        "tiles",
        (pltpu.VMEM((cols, cols), BF16), pltpu.VMEM((cols, cols), BF16), shape((modes, cols), BF16)),
        [VMEM_SPEC] * 3,
        [
            pltpu.VMEM((64, rows), F32),
            pltpu.VMEM((128, rows), F32),
            pltpu.VMEM((128, cols), BF16),
            pltpu.VMEM((128, cols), BF16),
            pltpu.VMEM((128, 256), BF16),
            pltpu.VMEM((modes, cols), F32),
        ],
        limit=32,
    )(own, other, edges)
    second, second_low = call(
        second_body,
        "second",
        (shape((modes, cols), F32), shape((modes, cols), BF16)),
        [VMEM_SPEC] * 6,
    )(panel_own, panel_other, filtered, lax.ppermute(filtered, "col", pair), own, edges)
    sums = call(functools.partial(image_body, float(rows)), "image", shape((modes, 128), F32), [VMEM_SPEC] * 5)(
        panel_own, panel_other, second_low, lax.ppermute(second_low, "col", pair), second
    )
    ritz, projected = call(
        functools.partial(ritz_body, ("fil", "col", col)),
        "ritz",
        (shape((modes, width), F32), shape((modes, modes), F32)),
        [VMEM_SPEC] * 3,
    )(sums, lax.ppermute(sums, "col", pair), second)
    return ritz.T, projected


def features(geometry, net_ids, layers):
    height = layers.astype(F32) * LAYER_PITCH
    return jnp.concatenate([geometry[0:2], height[None], geometry[2:6], net_ids.astype(F32)[None]], axis=0)


def kernel_tile(row_feat, col_feat, kernel_scale):
    delta_x = row_feat[0][:, None] - col_feat[0][None, :]
    delta_y = row_feat[1][:, None] - col_feat[1][None, :]
    delta_z = row_feat[2][:, None] - col_feat[2][None, :]
    radius_sq = (
        row_feat[6][:, None] * row_feat[6][:, None] + col_feat[6][None, :] * col_feat[6][None, :]
    )
    spread = delta_x * delta_x + delta_y * delta_y + delta_z * delta_z + radius_sq
    alignment = (
        row_feat[3][:, None] * col_feat[3][None, :]
        + row_feat[4][:, None] * col_feat[4][None, :]
        + row_feat[5][:, None] * col_feat[5][None, :]
    )
    couple = jnp.where(row_feat[7][:, None] == col_feat[7][None, :], 1.0, SHIELD_FACTOR)
    return (alignment * couple * lax.rsqrt(spread) * kernel_scale).astype(BF16)


def column_span(length, tile_rows, shard_rows):
    span_limit = max(shard_rows, (1 << 20) // tile_rows)
    span_cols = shard_rows
    while span_cols * 2 <= span_limit and length % (span_cols * 2) == 0:
        span_cols = span_cols * 2
    return span_cols


def accumulate(running, row_feat, part_feats, gathered, kernel_scale, span_cols):
    turns = gathered.shape[0] // span_cols

    def one_span(turn_index, partial_sum):
        offset = turn_index * span_cols
        span_feats = lax.dynamic_slice_in_dim(part_feats, offset, span_cols, 1)
        span_modes = lax.dynamic_slice_in_dim(gathered, offset, span_cols, 0)
        tile_vals = kernel_tile(row_feat, span_feats, kernel_scale)
        return partial_sum + jnp.dot(tile_vals, span_modes, preferred_element_type=F32)

    return lax.fori_loop(0, turns, one_span, running)


def general_shards(geometry, net_ids, layers, trial_modes, low_edge, high_edge):
    own_rows, modes_count = trial_modes.shape
    filaments = own_rows * lax.axis_size("fil") * lax.axis_size("col")
    kernel_scale = 1.0 / math.sqrt(filaments)
    own_feats = features(geometry, net_ids, layers)
    row_feat = lax.all_gather(own_feats, "col", axis=1, tiled=True)
    col_feat = lax.all_gather(own_feats, "fil", axis=1, tiled=True)
    tile_rows = row_feat.shape[1]

    def apply_operator(mode_block):
        gathered = lax.all_gather(mode_block, "fil", axis=0, tiled=True)
        initial = jnp.zeros((tile_rows, modes_count), F32)
        span = column_span(gathered.shape[0], tile_rows, own_rows)
        partial_value = accumulate(initial, row_feat, col_feat, gathered, kernel_scale, span)
        summed = lax.psum(partial_value, "col")
        return lax.dynamic_slice_in_dim(summed, lax.axis_index("col") * own_rows, own_rows, 0)

    centre = (low_edge[0] + high_edge[0]) * 0.5
    half_width = (high_edge[0] - low_edge[0]) * 0.5
    filtered_one = (
        (apply_operator(trial_modes) - centre * trial_modes.astype(F32)) / half_width
    ).astype(BF16)
    second = 2.0 * (
        apply_operator(filtered_one) - centre * filtered_one.astype(F32)
    ) / half_width - trial_modes.astype(F32)
    second_low = second.astype(BF16)
    gram_local = jnp.dot(second.T, second, precision=HIGHEST) / filaments
    image_block = apply_operator(second_low)
    cross_local = jnp.dot(second.T, image_block, precision=HIGHEST) / filaments
    gram_matrix, cross_matrix = lax.psum((gram_local, cross_local), ("fil", "col"))
    factor = jnp.linalg.cholesky(gram_matrix)
    ritz_basis = jax.scipy.linalg.solve_triangular(factor, second.T, lower=True).T
    half_solved = jax.scipy.linalg.solve_triangular(factor, cross_matrix, lower=True)
    projected = jax.scipy.linalg.solve_triangular(factor, half_solved.T, lower=True).T
    return (ritz_basis, projected)


def fits(mesh, width, modes):
    count = mesh.shape["fil"] * mesh.shape["col"]
    rows = count * width
    return (
        mesh.shape["col"] % 2 == 0
        and (count // 2) % 2 == 0
        and modes == 32
        and width == WIDTH
        and (rows // 2) % TILE_COLS == 0
        and (rows // 2) % TILE_ROWS == 0
        and rows * rows <= 16 * 1024 * 1024
    )


def solution(mesh):
    in_specs = (
        P(None, ("groups", "fil", "col")),
        P(("groups", "fil", "col")),
        P(("groups", "fil", "col")),
        P(("groups", "fil", "col"), None),
        P("groups"),
        P("groups"),
    )
    out_specs = (P(("groups", "fil", "col"), None), P("groups", None))

    def shards(geometry, net_ids, layers, trial_modes, low_edge, high_edge):
        form = paired_shards if fits(mesh, *trial_modes.shape) else general_shards
        return form(geometry, net_ids, layers, trial_modes, low_edge, high_edge)

    return jax.shard_map(shards, mesh=mesh, in_specs=in_specs, out_specs=out_specs, check_vma=False)
```

```python
import functools
import math

import jax
import jax.numpy as jnp
from jax import lax
from jax.experimental import pallas as pl
from jax.experimental.pallas import tpu as pltpu
from jax.sharding import PartitionSpec as P

SHIELD_FACTOR = 0.5
LAYER_PITCH = 0.02
NETS = 4
LAYERS = 8
F32 = jnp.float32
BF16 = jnp.bfloat16
HIGHEST = lax.Precision.HIGHEST
VMEM_SPEC = pl.BlockSpec(memory_space=pltpu.VMEM)
WIDTH = 192
TILE_ROWS = 512
TILE_COLS = 256


def pieces(x):
    high = x.astype(BF16).astype(F32)
    mid = (x - high).astype(BF16).astype(F32)
    low = (x - high - mid).astype(BF16).astype(F32)
    return high, mid, low


def pack_body(geometry, nets, layers, modes, out, *scratch):
    copies = []
    for index, source in enumerate((geometry, nets, layers, modes)):
        copies.append(pltpu.make_async_copy(source, scratch[index], scratch[4].at[index]))
        copies[-1].start()
    for copy in copies:
        copy.wait()
    geometry, nets, layers, modes, _, sheet = scratch
    high, mid, low = pieces(geometry[...])
    zeros = jnp.zeros((2, WIDTH), F32)
    rows = jnp.concatenate(
        [high, nets[...].astype(F32), layers[...].astype(F32), mid, zeros, low, zeros], axis=0
    )
    sheet[...] = jnp.zeros_like(sheet)
    sheet[0:32, 0:WIDTH] = modes[...].astype(F32)
    sheet[0:24, 192:256] = rows[:, 0:64]
    sheet[32:48, 0:64] = rows[0:16, 64:128]
    sheet[32:40, 64:128] = rows[16:24, 64:128]
    sheet[40:48, 64:128] = rows[0:8, 128:192]
    sheet[32:48, 128:192] = rows[8:24, 128:192]
    packed = sheet[...].astype(BF16)
    for place in range(out.shape[0]):
        out[place] = packed


def unpack(part, stage):
    for place in range(part.shape[0]):
        start = place * WIDTH
        sheet = part[place].astype(F32)
        stage[0:32, start : start + WIDTH] = sheet[0:32, 0:WIDTH]
        stage[32:56, start : start + 64] = sheet[0:24, 192:256]
        stage[32:48, start + 64 : start + 128] = sheet[32:48, 0:64]
        stage[48:56, start + 64 : start + 128] = sheet[32:40, 64:128]
        stage[32:40, start + 128 : start + 192] = sheet[40:48, 64:128]
        stage[40:56, start + 128 : start + 192] = sheet[32:48, 128:192]


def net_groups(base, nets):
    listed = [base] + [jnp.where(nets == float(n), base, 0.0) for n in range(NETS)]
    return jnp.concatenate(listed, axis=0)


def left_operand(stage, left):
    length = stage.shape[1]
    nets = stage[38:39, :]
    segment = [net_groups(stage[s + 2 : s + 5, :], nets) for s in (32, 40, 48)]
    place_x = [stage[s : s + 1, :] for s in (32, 40, 48)]
    place_y = [stage[s + 1 : s + 2, :] for s in (32, 40, 48)]
    spare = place_x + place_y
    for index, piece in enumerate((0, 0, 1, 1, 0, 2)):
        left[16 * index : 16 * index + 16, :] = jnp.concatenate([segment[piece], spare[index]], axis=0)
    levels = lax.broadcasted_iota(jnp.int32, (LAYERS, length), 0).astype(F32)
    chosen = jnp.where(levels == stage[39:40, :], 1.0, 0.0)
    left[96:104, :] = chosen
    left[104:112, :] = chosen
    left[112:120, :] = chosen
    ones = jnp.ones((3, length), F32)
    left[120:128, :] = jnp.concatenate([*squares(stage), ones, jnp.zeros((2, length), F32)], axis=0)


def squares(stage):
    return pieces(jnp.square(stage[37:38, :] + stage[45:46, :] + stage[53:54, :]))


def right_operand(scale, stage, right, coarse, places):
    cols = stage.shape[1]
    nets = stage[38:39, :]
    base = (stage[34:37, :] + stage[42:45, :] + stage[50:53, :]) * (SHIELD_FACTOR * scale)
    scaled = [net_groups(piece, nets) for piece in pieces(base)]
    blank = jnp.zeros((1, cols), F32)
    for index, piece in enumerate((0, 1, 0, 1, 2, 0)):
        right[16 * index : 16 * index + 16, :] = jnp.concatenate([scaled[piece], blank], axis=0).astype(BF16)
    right[96:128, :] = jnp.zeros((32, cols), BF16)
    coarse[0:96, :] = jnp.zeros((96, cols), BF16)
    levels = lax.broadcasted_iota(jnp.int32, (LAYERS, cols), 0).astype(F32)
    gap = levels * LAYER_PITCH - stage[39:40, :] * LAYER_PITCH
    ones = jnp.ones((3, cols), F32)
    coarse[96:128, :] = jnp.concatenate(
        [*pieces(gap * gap), ones, *squares(stage), jnp.zeros((2, cols), F32)], axis=0
    ).astype(BF16)
    places[...] = stage[32:40, :] + stage[40:48, :] + stage[48:56, :]


def place_columns():
    line = lax.broadcasted_iota(jnp.int32, (128, 256), 0)
    lane = lax.broadcasted_iota(jnp.int32, (128, 256), 1)
    for_x = (lane < 128) & ((line == 15) | (line == 31) | (line == 47))
    for_y = (lane >= 128) & ((line == 63) | (line == 79) | (line == 95))
    return jnp.where(for_x | for_y, 1.0, 0.0).astype(BF16)


def generate(left, right, coarse, places, panel, start):
    here = slice(start, start + TILE_ROWS)
    feats = left[:, here].T.astype(BF16)
    tall = jnp.dot(feats, place_columns(), preferred_element_type=F32)
    tall_x = jnp.concatenate([tall[:, 0:128]] * (TILE_COLS // 128), axis=1)
    tall_y = jnp.concatenate([tall[:, 128:256]] * (TILE_COLS // 128), axis=1)
    for first in range(0, panel.shape[1], TILE_COLS):
        there = slice(first, first + TILE_COLS)
        aligned = jnp.dot(feats, right[:, there], preferred_element_type=F32)
        spread = jnp.dot(feats, coarse[:, there], preferred_element_type=F32)
        delta_x = tall_x - places[0:1, there]
        delta_y = tall_y - places[1:2, there]
        spread = delta_x * delta_x + delta_y * delta_y + spread
        panel[here, there] = (aligned * lax.rsqrt(spread)).astype(BF16)


def partial_product(modes, panel, start):
    here = slice(start, start + TILE_ROWS)
    return jnp.dot(modes[:, here], panel[here, :], preferred_element_type=F32)


def own_tiles_body(scale, own, panel, right, coarse, places, modes, total, stage, left):
    unpack(own, stage)
    left_operand(stage, left)
    right_operand(scale, stage, right, coarse, places)
    modes[...] = stage[0:32, :].astype(BF16)
    cols = panel.shape[0]
    generate(left, right, coarse, places, panel, 0)
    for start in range(TILE_ROWS, cols, TILE_ROWS):
        done = partial_product(modes, panel, start - TILE_ROWS)
        total[...] = done if start == TILE_ROWS else total[...] + done
        generate(left, right, coarse, places, panel, start)
    total[...] += partial_product(modes, panel, cols - TILE_ROWS)


def other_tiles_body(other, right, coarse, places, modes, total, low_edge, high_edge, panel, filtered, stage, left, others):
    unpack(other, stage)
    left_operand(stage, left)
    others[...] = stage[0:32, :].astype(BF16)
    cols = panel.shape[0]
    applied = total[...]
    generate(left, right, coarse, places, panel, 0)
    for start in range(TILE_ROWS, cols, TILE_ROWS):
        applied = applied + partial_product(others, panel, start - TILE_ROWS)
        generate(left, right, coarse, places, panel, start)
    applied = applied + partial_product(others, panel, cols - TILE_ROWS)
    centre = (low_edge[...] + high_edge[...]) * 0.5
    half_width = (high_edge[...] - low_edge[...]) * 0.5
    filtered[...] = ((applied - centre * modes[...].astype(F32)) / half_width).astype(BF16)


def half_body(panel, own, part):
    part[...] = jnp.dot(own[...], panel[...], preferred_element_type=F32)


def second_body(panel, other, part, own, modes, low_edge, high_edge, second, second_low):
    applied = part[...] + jnp.dot(other[...], panel[...], preferred_element_type=F32)
    centre = (low_edge[...] + high_edge[...]) * 0.5
    half_width = (high_edge[...] - low_edge[...]) * 0.5
    value = 2.0 * (applied - centre * own[...].astype(F32)) / half_width - modes[...].astype(F32)
    second[...] = value
    second_low[...] = value.astype(BF16)


def outer(a, b):
    return lax.dot_general(a, b, (((1,), (1,)), ((), ())), precision=HIGHEST, preferred_element_type=F32)


def gram_body(filaments, second, gram):
    gram[...] = outer(second[...], second[...]) / filaments


def image_body(filaments, panel, other, part, second, gram, gram_other, cross, inverse):
    modes = gram.shape[0]
    line = lax.broadcasted_iota(jnp.int32, (modes, modes), 0)
    lane = lax.broadcasted_iota(jnp.int32, (modes, modes), 1)
    unit = jnp.where(lane == line, 1.0, 0.0)
    system = jnp.concatenate([gram[...] + gram_other[...], unit], axis=1)
    applied = part[...] + jnp.dot(other[...], panel[...], preferred_element_type=F32)
    cross[...] = outer(second[...], applied) / filaments
    for pivot in range(modes):
        row = system[pivot : pivot + 1, :]
        column = system[:, pivot : pivot + 1] / system[pivot : pivot + 1, pivot : pivot + 1]
        column = jnp.where(line[:, 0:1] > pivot, column, 0.0)
        system = system - column * row
    diagonal = jnp.sum(system[:, 0:modes] * unit, axis=1, keepdims=True)
    inverse[...] = system[:, modes : 2 * modes] / jnp.sqrt(diagonal)


def ritz_body(axes, inverse, second, ritz):
    width = ritz.shape[1]
    fil, col, col_size = axes
    place = lax.axis_index(fil) * (col_size // 2) + lax.axis_index(col) // 2
    odd = place % 2
    start = (place // 2) * (2 * width) + odd * (width - 64)
    window = second[:, pl.ds(pl.multiple_of(start, 128), width + 64)]
    moved = pltpu.roll(window, width, 1)
    mine = jnp.where(odd == 1, moved, window)[:, 0:width]
    ritz[...] = jnp.dot(inverse[...], mine, precision=HIGHEST, preferred_element_type=F32)


def projected_body(inverse, cross, cross_other, projected):
    half_solved = jnp.dot(
        inverse[...], cross[...] + cross_other[...], precision=HIGHEST, preferred_element_type=F32
    )
    projected[...] = outer(half_solved, inverse[...])


def call(body, name, out_shape, in_specs, scratch=(), limit=16, work=0):
    return pl.pallas_call(
        body,
        name=name,
        out_shape=out_shape,
        in_specs=in_specs,
        out_specs=jax.tree.map(lambda _: VMEM_SPEC, out_shape),
        scratch_shapes=list(scratch),
        compiler_params=pltpu.CompilerParams(vmem_limit_bytes=limit * 1024 * 1024),
        cost_estimate=pl.CostEstimate(flops=2 * work, bytes_accessed=0, transcendentals=0) if work else None,
    )


def paired_shards(geometry, net_ids, layers, trial_modes, low_edge, high_edge):
    width, modes = trial_modes.shape
    fil, col = lax.axis_size("fil"), lax.axis_size("col")
    count = fil * col // 2
    cols = count * width
    rows = 2 * cols
    shape = jax.ShapeDtypeStruct
    pair = [(i, i ^ 1) for i in range(col)]
    same_core = [[2 * chip + core for chip in range(count)] for core in range(2)]

    packed = call(
        pack_body,
        "pack",
        shape((count, 48, 256), BF16),
        [pl.BlockSpec(memory_space=pl.ANY)] * 4,
        [
            pltpu.VMEM(geometry.shape, F32),
            pltpu.VMEM((1, width), jnp.int32),
            pltpu.VMEM((1, width), jnp.int32),
            pltpu.VMEM((modes, width), BF16),
            pltpu.SemaphoreType.DMA((4,)),
            pltpu.VMEM((48, 256), F32),
        ],
    )(
        *(
            pltpu.with_memory_space_constraint(x, pltpu.HBM)
            for x in (
                geometry,
                net_ids.reshape(1, width),
                layers.reshape(1, width),
                trial_modes.T,
            )
        )
    )
    edges = (low_edge.reshape(1, 1), high_edge.reshape(1, 1))
    own = lax.all_to_all(packed, ("fil", "col"), 0, 0, axis_index_groups=same_core, tiled=True)
    other = lax.ppermute(own, "col", pair)
    square = pltpu.VMEM((cols, cols), BF16)
    operand = shape((128, cols), BF16)
    stages = [pltpu.VMEM((64, cols), F32), pltpu.VMEM((128, cols), F32)]
    panel_own, right, coarse, places, low, total = call(
        functools.partial(own_tiles_body, 1.0 / math.sqrt(rows)),
        "own_tiles",
        (square, operand, operand, shape((8, cols), F32), shape((modes, cols), BF16), shape((modes, cols), F32)),
        [VMEM_SPEC],
        stages,
        work=cols * cols * 160,
    )(own)
    panel_other, filtered = call(
        other_tiles_body,
        "other_tiles",
        (square, shape((modes, cols), BF16)),
        [VMEM_SPEC] * 8,
        [*stages, pltpu.VMEM((modes, cols), BF16)],
        work=cols * cols * 160,
    )(other, right, coarse, places, low, total, *edges)

    half = call(half_body, "half", shape((modes, cols), F32), [VMEM_SPEC] * 2, work=cols * cols * modes)
    filtered_other = lax.ppermute(filtered, "col", pair)
    second, second_low = call(
        second_body,
        "second",
        (shape((modes, cols), F32), shape((modes, cols), BF16)),
        [VMEM_SPEC] * 7,
    )(panel_other, filtered_other, half(panel_own, filtered), filtered, low, *edges)
    second_other = lax.ppermute(second_low, "col", pair)
    gram = call(functools.partial(gram_body, float(rows)), "gram", shape((modes, modes), F32), [VMEM_SPEC])(second)
    gram_other = lax.ppermute(gram, "col", pair)
    cross, inverse = call(
        functools.partial(image_body, float(rows)),
        "image",
        (shape((modes, modes), F32), shape((modes, modes), F32)),
        [VMEM_SPEC] * 6,
    )(panel_other, second_other, half(panel_own, second_low), second, gram, gram_other)
    cross_other = lax.ppermute(cross, "col", pair)
    ritz = call(
        functools.partial(ritz_body, ("fil", "col", col)), "ritz", shape((modes, width), F32), [VMEM_SPEC] * 2
    )(inverse, second)
    projected = call(projected_body, "projected", shape((modes, modes), F32), [VMEM_SPEC] * 3)(
        inverse, cross, cross_other
    )
    return ritz.T, projected


def features(geometry, net_ids, layers):
    height = layers.astype(F32) * LAYER_PITCH
    return jnp.concatenate([geometry[0:2], height[None], geometry[2:6], net_ids.astype(F32)[None]], axis=0)


def kernel_tile(row_feat, col_feat, kernel_scale):
    delta_x = row_feat[0][:, None] - col_feat[0][None, :]
    delta_y = row_feat[1][:, None] - col_feat[1][None, :]
    delta_z = row_feat[2][:, None] - col_feat[2][None, :]
    radius_sq = (
        row_feat[6][:, None] * row_feat[6][:, None] + col_feat[6][None, :] * col_feat[6][None, :]
    )
    spread = delta_x * delta_x + delta_y * delta_y + delta_z * delta_z + radius_sq
    alignment = (
        row_feat[3][:, None] * col_feat[3][None, :]
        + row_feat[4][:, None] * col_feat[4][None, :]
        + row_feat[5][:, None] * col_feat[5][None, :]
    )
    couple = jnp.where(row_feat[7][:, None] == col_feat[7][None, :], 1.0, SHIELD_FACTOR)
    return (alignment * couple * lax.rsqrt(spread) * kernel_scale).astype(BF16)


def column_span(length, tile_rows, shard_rows):
    span_limit = max(shard_rows, (1 << 20) // tile_rows)
    span_cols = shard_rows
    while span_cols * 2 <= span_limit and length % (span_cols * 2) == 0:
        span_cols = span_cols * 2
    return span_cols


def accumulate(running, row_feat, part_feats, gathered, kernel_scale, span_cols):
    turns = gathered.shape[0] // span_cols

    def one_span(turn_index, partial_sum):
        offset = turn_index * span_cols
        span_feats = lax.dynamic_slice_in_dim(part_feats, offset, span_cols, 1)
        span_modes = lax.dynamic_slice_in_dim(gathered, offset, span_cols, 0)
        tile_vals = kernel_tile(row_feat, span_feats, kernel_scale)
        return partial_sum + jnp.dot(tile_vals, span_modes, preferred_element_type=F32)

    return lax.fori_loop(0, turns, one_span, running)


def general_shards(geometry, net_ids, layers, trial_modes, low_edge, high_edge):
    own_rows, modes_count = trial_modes.shape
    filaments = own_rows * lax.axis_size("fil") * lax.axis_size("col")
    kernel_scale = 1.0 / math.sqrt(filaments)
    own_feats = features(geometry, net_ids, layers)
    row_feat = lax.all_gather(own_feats, "col", axis=1, tiled=True)
    col_feat = lax.all_gather(own_feats, "fil", axis=1, tiled=True)
    tile_rows = row_feat.shape[1]

    def apply_operator(mode_block):
        gathered = lax.all_gather(mode_block, "fil", axis=0, tiled=True)
        initial = jnp.zeros((tile_rows, modes_count), F32)
        span = column_span(gathered.shape[0], tile_rows, own_rows)
        partial_value = accumulate(initial, row_feat, col_feat, gathered, kernel_scale, span)
        summed = lax.psum(partial_value, "col")
        return lax.dynamic_slice_in_dim(summed, lax.axis_index("col") * own_rows, own_rows, 0)

    centre = (low_edge[0] + high_edge[0]) * 0.5
    half_width = (high_edge[0] - low_edge[0]) * 0.5
    filtered_one = (
        (apply_operator(trial_modes) - centre * trial_modes.astype(F32)) / half_width
    ).astype(BF16)
    second = 2.0 * (
        apply_operator(filtered_one) - centre * filtered_one.astype(F32)
    ) / half_width - trial_modes.astype(F32)
    second_low = second.astype(BF16)
    gram_local = jnp.dot(second.T, second, precision=HIGHEST) / filaments
    image_block = apply_operator(second_low)
    cross_local = jnp.dot(second.T, image_block, precision=HIGHEST) / filaments
    gram_matrix, cross_matrix = lax.psum((gram_local, cross_local), ("fil", "col"))
    factor = jnp.linalg.cholesky(gram_matrix)
    ritz_basis = jax.scipy.linalg.solve_triangular(factor, second.T, lower=True).T
    half_solved = jax.scipy.linalg.solve_triangular(factor, cross_matrix, lower=True)
    projected = jax.scipy.linalg.solve_triangular(factor, half_solved.T, lower=True).T
    return (ritz_basis, projected)


def fits(mesh, width, modes):
    count = mesh.shape["fil"] * mesh.shape["col"]
    rows = count * width
    return (
        mesh.shape["col"] % 2 == 0
        and (count // 2) % 2 == 0
        and modes == 32
        and width == WIDTH
        and (rows // 2) % TILE_COLS == 0
        and (rows // 2) % TILE_ROWS == 0
        and rows * rows <= 16 * 1024 * 1024
    )


def solution(mesh):
    in_specs = (
        P(None, ("groups", "fil", "col")),
        P(("groups", "fil", "col")),
        P(("groups", "fil", "col")),
        P(("groups", "fil", "col"), None),
        P("groups"),
        P("groups"),
    )
    out_specs = (P(("groups", "fil", "col"), None), P("groups", None))

    def shards(geometry, net_ids, layers, trial_modes, low_edge, high_edge):
        form = paired_shards if fits(mesh, *trial_modes.shape) else general_shards
        return form(geometry, net_ids, layers, trial_modes, low_edge, high_edge)

    return jax.shard_map(shards, mesh=mesh, in_specs=in_specs, out_specs=out_specs, check_vma=False)
```

```python
import functools
import math

import jax
import jax.numpy as jnp
from jax import lax
from jax.experimental import pallas as pl
from jax.experimental.pallas import tpu as pltpu
from jax.sharding import PartitionSpec as P

SHIELD_FACTOR = 0.5
LAYER_PITCH = 0.02
NETS = 4
LAYERS = 8
F32 = jnp.float32
BF16 = jnp.bfloat16
HIGHEST = lax.Precision.HIGHEST
VMEM_SPEC = pl.BlockSpec(memory_space=pltpu.VMEM)
WIDTH = 192
CHUNK = 256
TALL = 256
PIVOTS = 8


def pieces(x):
    high = x.astype(BF16).astype(F32)
    mid = (x - high).astype(BF16).astype(F32)
    low = (x - high - mid).astype(BF16).astype(F32)
    return high, mid, low


def pack_body(geometry, nets, layers, modes, out, *scratch):
    copies = []
    for index, source in enumerate((geometry, nets, layers, modes)):
        copies.append(pltpu.make_async_copy(source, scratch[index], scratch[4].at[index]))
        copies[-1].start()
    for copy in copies:
        copy.wait()
    geometry, nets, layers, modes, _, sheet = scratch
    high, mid, low = pieces(geometry[...])
    rows = jnp.concatenate(
        [
            *(high[2:5], mid[2:5], high[0:2]),
            *(high[2:5], low[2:5], mid[0:2]),
            *(low[0:2], high[5:6], mid[5:6], low[5:6]),
            *(nets[...].astype(F32), layers[...].astype(F32), jnp.zeros((1, WIDTH), F32)),
        ],
        axis=0,
    )
    sheet[...] = jnp.zeros_like(sheet)
    sheet[0:32, 0:WIDTH] = modes[...].astype(F32)
    sheet[0:24, 192:256] = rows[:, 0:64]
    sheet[32:48, 0:64] = rows[0:16, 64:128]
    sheet[32:40, 64:128] = rows[16:24, 64:128]
    sheet[40:48, 64:128] = rows[0:8, 128:192]
    sheet[32:48, 128:192] = rows[8:24, 128:192]
    packed = sheet[...].astype(BF16)
    for place in range(out.shape[0]):
        out[place] = packed


def unpack(part, stage):
    for place in range(part.shape[0]):
        start = place * WIDTH
        sheet = part[place].astype(F32)
        stage[0:32, start : start + WIDTH] = sheet[0:32, 0:WIDTH]
        stage[32:56, start : start + 64] = sheet[0:24, 192:256]
        stage[32:48, start + 64 : start + 128] = sheet[32:48, 0:64]
        stage[48:56, start + 64 : start + 128] = sheet[32:40, 64:128]
        stage[32:40, start + 128 : start + 192] = sheet[40:48, 64:128]
        stage[40:56, start + 128 : start + 192] = sheet[32:48, 128:192]


def signs(stage):
    net = stage[53:54, :]
    upper = jnp.where(net >= 2.0, 1.0, 0.0)
    a = 1.0 - 2.0 * (net - 2.0 * upper)
    b = 1.0 - 2.0 * upper
    return a, b, a * b


def squares(stage):
    return pieces(jnp.square(stage[50:51, :] + stage[51:52, :] + stage[52:53, :]))


def left_operand(stage, left, feats, tall):
    length = stage.shape[1]
    base = stage[32:40, :]
    fine = stage[40:48, :]
    left[0:8, :] = base
    left[32:40, :] = base
    left[64:72, :] = fine
    for index, sign in enumerate(signs(stage)):
        at = 8 * index + 8
        signed = base * sign
        left[at : at + 8, :] = signed
        left[32 + at : 40 + at, :] = signed
        left[64 + at : 72 + at, :] = fine * sign
    levels = lax.broadcasted_iota(jnp.int32, (LAYERS, length), 0).astype(F32)
    chosen = jnp.where(levels == stage[54:55, :], 1.0, 0.0)
    left[96:104, :] = chosen
    left[104:112, :] = chosen
    left[112:120, :] = chosen
    left[120:128, :] = jnp.concatenate([*squares(stage), jnp.ones((3, length), F32), stage[48:50, :]], axis=0)
    line = lax.broadcasted_iota(jnp.int32, (128, 256), 0)
    lane = lax.broadcasted_iota(jnp.int32, (128, 256), 1)
    for_x = (lane < 128) & ((line == 6) | (line == 70) | (line == 126))
    for_y = (lane >= 128) & ((line == 7) | (line == 71) | (line == 127))
    columns = jnp.where(for_x | for_y, 1.0, 0.0).astype(BF16)
    for start in range(0, length, CHUNK):
        here = slice(start, start + CHUNK)
        turned = left[:, here].T.astype(BF16)
        feats[here, :] = turned
        tall[here, :] = jnp.dot(turned, columns, preferred_element_type=F32)


def right_operand(scale, stage, right, coarse, places):
    cols = stage.shape[1]
    rest = (1.0 - SHIELD_FACTOR) / NETS
    segment = stage[32:35, :] + stage[35:38, :] + stage[43:46, :]
    blank = jnp.zeros((2, cols), F32)

    def blocks(weight):
        high, mid, low = pieces(segment * weight)
        return [jnp.concatenate(pair, axis=0) for pair in ((high, mid, blank), (mid, high, blank), (low, high, blank))]

    plain = blocks((SHIELD_FACTOR + rest) * scale)
    extra = blocks(rest * scale)
    for index in range(3):
        signed = [extra[index] * sign for sign in signs(stage)]
        right[32 * index : 32 * index + 32, :] = jnp.concatenate([plain[index], *signed], axis=0).astype(BF16)
    right[96:128, :] = jnp.zeros((32, cols), BF16)
    coarse[0:96, :] = jnp.zeros((96, cols), BF16)
    levels = lax.broadcasted_iota(jnp.int32, (LAYERS, cols), 0).astype(F32)
    gap = levels * LAYER_PITCH - stage[54:55, :] * LAYER_PITCH
    coarse[96:128, :] = jnp.concatenate(
        [*pieces(gap * gap), jnp.ones((3, cols), F32), *squares(stage), blank], axis=0
    ).astype(BF16)
    places[0:2, :] = stage[38:40, :] + stage[46:48, :] + stage[48:50, :]
    places[2:8, :] = jnp.zeros((6, cols), F32)


def generate(feats, tall, right, coarse, places, panel, first, start):
    for top in range(first, panel.shape[0], TALL):
        generate_rows(feats, tall, right, coarse, places, panel, slice(top, min(top + TALL, panel.shape[0])), start)


def generate_rows(feats, tall, right, coarse, places, panel, here, start):
    there = slice(start, start + CHUNK)
    rows = feats[here, :]
    aligned = jnp.dot(rows, right[:, there], preferred_element_type=F32)
    spread = jnp.dot(rows, coarse[:, there], preferred_element_type=F32)
    tall_x = jnp.concatenate([tall[here, 0:128]] * (CHUNK // 128), axis=1)
    tall_y = jnp.concatenate([tall[here, 128:256]] * (CHUNK // 128), axis=1)
    delta_x = tall_x - places[0:1, there]
    delta_y = tall_y - places[1:2, there]
    spread = delta_x * delta_x + delta_y * delta_y + spread
    panel[here, there] = (aligned * lax.rsqrt(spread)).astype(BF16)


def own_tiles_body(scale, own, panel, right, coarse, places, modes, total, stage, left, feats, tall):
    unpack(own, stage)
    left_operand(stage, left, feats, tall)
    right_operand(scale, stage, right, coarse, places)
    modes[...] = stage[0:32, :].astype(BF16)
    cols = panel.shape[0]

    def multiply(start):
        there = slice(start, start + CHUNK)
        total[:, there] = jnp.dot(modes[...], panel[:, there], preferred_element_type=F32)

    for start in range(0, cols, CHUNK):
        if start > 0:
            multiply(start - CHUNK)
        generate(feats, tall, right, coarse, places, panel, start, start)
        there = slice(start, start + CHUNK)
        for other in range(0, start, CHUNK):
            panel[other : other + CHUNK, there] = panel[there, other : other + CHUNK].T
    multiply(cols - CHUNK)


def other_tiles_body(other, right, coarse, places, modes, total, low_edge, high_edge, panel, filtered, *scratch):
    stage, left, feats, tall, others = scratch
    unpack(other, stage)
    left_operand(stage, left, feats, tall)
    others[...] = stage[0:32, :].astype(BF16)
    cols = panel.shape[0]
    centre = (low_edge[...] + high_edge[...]) * 0.5
    half_width = (high_edge[...] - low_edge[...]) * 0.5

    def multiply(start):
        there = slice(start, start + CHUNK)
        applied = total[:, there] + jnp.dot(others[...], panel[:, there], preferred_element_type=F32)
        filtered[:, there] = ((applied - centre * modes[:, there].astype(F32)) / half_width).astype(BF16)

    for start in range(0, cols, CHUNK):
        if start > 0:
            multiply(start - CHUNK)
        generate(feats, tall, right, coarse, places, panel, 0, start)
    multiply(cols - CHUNK)


def half_body(panel, own, part):
    part[...] = jnp.dot(own[...], panel[...], preferred_element_type=F32)


def second_body(panel, other, part, own, modes, low_edge, high_edge, second, second_low):
    applied = part[...] + jnp.dot(other[...], panel[...], preferred_element_type=F32)
    centre = (low_edge[...] + high_edge[...]) * 0.5
    half_width = (high_edge[...] - low_edge[...]) * 0.5
    value = 2.0 * (applied - centre * own[...].astype(F32)) / half_width - modes[...].astype(F32)
    second[...] = value
    second_low[...] = value.astype(BF16)


def outer(a, b):
    return lax.dot_general(a, b, (((1,), (1,)), ((), ())), precision=HIGHEST, preferred_element_type=F32)


def gram_body(filaments, second, gram):
    gram[...] = outer(second[...], second[...]) / filaments


def eliminate(system, modes):
    line = lax.broadcasted_iota(jnp.int32, system.shape, 0)
    for first in range(0, modes, PIVOTS):
        step = range(first, first + PIVOTS)
        columns = {k: jnp.broadcast_to(system[:, k : k + 1], system.shape) for k in step}
        rows = {k: system[k : k + 1, :] for k in step}
        weights = {}
        for k in step:
            weights[k] = jnp.where(line > k, columns[k] / columns[k][k : k + 1, :], 0.0)
            for later in range(k + 1, first + PIVOTS):
                columns[later] = columns[later] - weights[k] * columns[k][later : later + 1, :]
                rows[later] = rows[later] - weights[k][later : later + 1, :] * rows[k]
        for k in step:
            system = system - weights[k] * rows[k]
    return system


def image_body(filaments, panel, other, part, second, gram, gram_other, cross, inverse):
    modes = gram.shape[0]
    line = lax.broadcasted_iota(jnp.int32, (modes, modes), 0)
    lane = lax.broadcasted_iota(jnp.int32, (modes, modes), 1)
    unit = jnp.where(lane == line, 1.0, 0.0)
    system = jnp.concatenate([gram[...] + gram_other[...], unit, unit, unit], axis=1)
    applied = part[...] + jnp.dot(other[...], panel[...], preferred_element_type=F32)
    cross[...] = outer(second[...], applied) / filaments
    system = eliminate(system, modes)
    diagonal = jnp.sum(system[:, 0:modes] * unit, axis=1, keepdims=True)
    inverse[...] = system[:, modes : 2 * modes] / jnp.sqrt(diagonal)


def ritz_body(axes, inverse, second, ritz):
    width = ritz.shape[1]
    fil, col, col_size = axes
    place = lax.axis_index(fil) * (col_size // 2) + lax.axis_index(col) // 2
    odd = place % 2
    start = (place // 2) * (2 * width) + odd * (width - 64)
    window = second[:, pl.ds(pl.multiple_of(start, 128), width + 64)]
    moved = pltpu.roll(window, width, 1)
    mine = jnp.where(odd == 1, moved, window)[:, 0:width]
    ritz[...] = jnp.dot(inverse[...], mine, precision=HIGHEST, preferred_element_type=F32)


def projected_body(inverse, cross, cross_other, projected):
    half_solved = jnp.dot(
        inverse[...], cross[...] + cross_other[...], precision=HIGHEST, preferred_element_type=F32
    )
    projected[...] = outer(half_solved, inverse[...])


def call(body, name, out_shape, in_specs, scratch=(), limit=16, work=0):
    return pl.pallas_call(
        body,
        name=name,
        out_shape=out_shape,
        in_specs=in_specs,
        out_specs=jax.tree.map(lambda _: VMEM_SPEC, out_shape),
        scratch_shapes=list(scratch),
        compiler_params=pltpu.CompilerParams(vmem_limit_bytes=limit * 1024 * 1024),
        cost_estimate=pl.CostEstimate(flops=2 * work, bytes_accessed=0, transcendentals=0) if work else None,
    )


def paired_shards(geometry, net_ids, layers, trial_modes, low_edge, high_edge):
    width, modes = trial_modes.shape
    fil, col = lax.axis_size("fil"), lax.axis_size("col")
    count = fil * col // 2
    cols = count * width
    rows = 2 * cols
    shape = jax.ShapeDtypeStruct
    pair = [(i, i ^ 1) for i in range(col)]
    same_core = [[2 * chip + core for chip in range(count)] for core in range(2)]

    packed = call(
        pack_body,
        "pack",
        shape((count, 48, 256), BF16),
        [pl.BlockSpec(memory_space=pl.ANY)] * 4,
        [
            pltpu.VMEM(geometry.shape, F32),
            pltpu.VMEM((1, width), jnp.int32),
            pltpu.VMEM((1, width), jnp.int32),
            pltpu.VMEM((modes, width), BF16),
            pltpu.SemaphoreType.DMA((4,)),
            pltpu.VMEM((48, 256), F32),
        ],
    )(
        *(
            pltpu.with_memory_space_constraint(x, pltpu.HBM)
            for x in (
                geometry,
                net_ids.reshape(1, width),
                layers.reshape(1, width),
                trial_modes.T,
            )
        )
    )
    edges = (low_edge.reshape(1, 1), high_edge.reshape(1, 1))
    own = lax.all_to_all(packed, ("fil", "col"), 0, 0, axis_index_groups=same_core, tiled=True)
    other = lax.ppermute(own, "col", pair)
    square = pltpu.VMEM((cols, cols), BF16)
    operand = shape((128, cols), BF16)
    stages = [
        pltpu.VMEM((56, cols), F32),
        pltpu.VMEM((128, cols), F32),
        pltpu.VMEM((cols, 128), BF16),
        pltpu.VMEM((cols, 256), F32),
    ]
    panel_own, right, coarse, places, low, total = call(
        functools.partial(own_tiles_body, 1.0 / math.sqrt(rows)),
        "own_tiles",
        (square, operand, operand, shape((8, cols), F32), shape((modes, cols), BF16), shape((modes, cols), F32)),
        [VMEM_SPEC],
        stages,
        work=cols * cols * 160,
    )(own)
    panel_other, filtered = call(
        other_tiles_body,
        "other_tiles",
        (square, shape((modes, cols), BF16)),
        [VMEM_SPEC] * 8,
        [*stages, pltpu.VMEM((modes, cols), BF16)],
        work=cols * cols * 160,
    )(other, right, coarse, places, low, total, *edges)

    half = call(half_body, "half", shape((modes, cols), F32), [VMEM_SPEC] * 2, work=cols * cols * modes)
    filtered_other = lax.ppermute(filtered, "col", pair)
    second, second_low = call(
        second_body,
        "second",
        (shape((modes, cols), F32), shape((modes, cols), BF16)),
        [VMEM_SPEC] * 7,
    )(panel_other, filtered_other, half(panel_own, filtered), filtered, low, *edges)
    second_other = lax.ppermute(second_low, "col", pair)
    gram = call(functools.partial(gram_body, float(rows)), "gram", shape((modes, modes), F32), [VMEM_SPEC])(second)
    gram_other = lax.ppermute(gram, "col", pair)
    cross, inverse = call(
        functools.partial(image_body, float(rows)),
        "image",
        (shape((modes, modes), F32), shape((modes, modes), F32)),
        [VMEM_SPEC] * 6,
    )(panel_other, second_other, half(panel_own, second_low), second, gram, gram_other)
    cross_other = lax.ppermute(cross, "col", pair)
    ritz = call(
        functools.partial(ritz_body, ("fil", "col", col)), "ritz", shape((modes, width), F32), [VMEM_SPEC] * 2
    )(inverse, second)
    projected = call(projected_body, "projected", shape((modes, modes), F32), [VMEM_SPEC] * 3)(
        inverse, cross, cross_other
    )
    return ritz.T, projected


def features(geometry, net_ids, layers):
    height = layers.astype(F32) * LAYER_PITCH
    return jnp.concatenate([geometry[0:2], height[None], geometry[2:6], net_ids.astype(F32)[None]], axis=0)


def kernel_tile(row_feat, col_feat, kernel_scale):
    delta_x = row_feat[0][:, None] - col_feat[0][None, :]
    delta_y = row_feat[1][:, None] - col_feat[1][None, :]
    delta_z = row_feat[2][:, None] - col_feat[2][None, :]
    radius_sq = (
        row_feat[6][:, None] * row_feat[6][:, None] + col_feat[6][None, :] * col_feat[6][None, :]
    )
    spread = delta_x * delta_x + delta_y * delta_y + delta_z * delta_z + radius_sq
    alignment = (
        row_feat[3][:, None] * col_feat[3][None, :]
        + row_feat[4][:, None] * col_feat[4][None, :]
        + row_feat[5][:, None] * col_feat[5][None, :]
    )
    couple = jnp.where(row_feat[7][:, None] == col_feat[7][None, :], 1.0, SHIELD_FACTOR)
    return (alignment * couple * lax.rsqrt(spread) * kernel_scale).astype(BF16)


def column_span(length, tile_rows, shard_rows):
    span_limit = max(shard_rows, (1 << 20) // tile_rows)
    span_cols = shard_rows
    while span_cols * 2 <= span_limit and length % (span_cols * 2) == 0:
        span_cols = span_cols * 2
    return span_cols


def accumulate(running, row_feat, part_feats, gathered, kernel_scale, span_cols):
    turns = gathered.shape[0] // span_cols

    def one_span(turn_index, partial_sum):
        offset = turn_index * span_cols
        span_feats = lax.dynamic_slice_in_dim(part_feats, offset, span_cols, 1)
        span_modes = lax.dynamic_slice_in_dim(gathered, offset, span_cols, 0)
        tile_vals = kernel_tile(row_feat, span_feats, kernel_scale)
        return partial_sum + jnp.dot(tile_vals, span_modes, preferred_element_type=F32)

    return lax.fori_loop(0, turns, one_span, running)


def general_shards(geometry, net_ids, layers, trial_modes, low_edge, high_edge):
    own_rows, modes_count = trial_modes.shape
    filaments = own_rows * lax.axis_size("fil") * lax.axis_size("col")
    kernel_scale = 1.0 / math.sqrt(filaments)
    own_feats = features(geometry, net_ids, layers)
    row_feat = lax.all_gather(own_feats, "col", axis=1, tiled=True)
    col_feat = lax.all_gather(own_feats, "fil", axis=1, tiled=True)
    tile_rows = row_feat.shape[1]

    def apply_operator(mode_block):
        gathered = lax.all_gather(mode_block, "fil", axis=0, tiled=True)
        initial = jnp.zeros((tile_rows, modes_count), F32)
        span = column_span(gathered.shape[0], tile_rows, own_rows)
        partial_value = accumulate(initial, row_feat, col_feat, gathered, kernel_scale, span)
        summed = lax.psum(partial_value, "col")
        return lax.dynamic_slice_in_dim(summed, lax.axis_index("col") * own_rows, own_rows, 0)

    centre = (low_edge[0] + high_edge[0]) * 0.5
    half_width = (high_edge[0] - low_edge[0]) * 0.5
    filtered_one = (
        (apply_operator(trial_modes) - centre * trial_modes.astype(F32)) / half_width
    ).astype(BF16)
    second = 2.0 * (
        apply_operator(filtered_one) - centre * filtered_one.astype(F32)
    ) / half_width - trial_modes.astype(F32)
    second_low = second.astype(BF16)
    gram_local = jnp.dot(second.T, second, precision=HIGHEST) / filaments
    image_block = apply_operator(second_low)
    cross_local = jnp.dot(second.T, image_block, precision=HIGHEST) / filaments
    gram_matrix, cross_matrix = lax.psum((gram_local, cross_local), ("fil", "col"))
    factor = jnp.linalg.cholesky(gram_matrix)
    ritz_basis = jax.scipy.linalg.solve_triangular(factor, second.T, lower=True).T
    half_solved = jax.scipy.linalg.solve_triangular(factor, cross_matrix, lower=True)
    projected = jax.scipy.linalg.solve_triangular(factor, half_solved.T, lower=True).T
    return (ritz_basis, projected)


def fits(mesh, width, modes):
    count = mesh.shape["fil"] * mesh.shape["col"]
    rows = count * width
    return (
        mesh.shape["col"] % 2 == 0
        and (count // 2) % 2 == 0
        and modes == 32
        and width == WIDTH
        and (rows // 2) % CHUNK == 0
        and rows * rows <= 16 * 1024 * 1024
    )


def solution(mesh):
    in_specs = (
        P(None, ("groups", "fil", "col")),
        P(("groups", "fil", "col")),
        P(("groups", "fil", "col")),
        P(("groups", "fil", "col"), None),
        P("groups"),
        P("groups"),
    )
    out_specs = (P(("groups", "fil", "col"), None), P("groups", None))

    def shards(geometry, net_ids, layers, trial_modes, low_edge, high_edge):
        form = paired_shards if fits(mesh, *trial_modes.shape) else general_shards
        return form(geometry, net_ids, layers, trial_modes, low_edge, high_edge)

    return jax.shard_map(shards, mesh=mesh, in_specs=in_specs, out_specs=out_specs, check_vma=False)
```
